256 devices in a mesh: tomo: 8 (over z), tilt: 32 (over y, x, core).
Axes of the slice: x: 4, y: 4, z: 8, core: 2. Of those that a mesh axis runs over, the one named last changes fastest.
Arguments:
- tilt_images: bfloat16 [8, 32, 1024, 1024], P('tomo', 'tilt'), may hold values from -6 to 6
- anchors: int32 [8, 32, 32, 2], P('tomo', 'tilt'), may hold values from 0 to 960
- euler: float32 [8, 3, 32], P('tomo'), may hold values from -3.140625 to 3.140625
- tilt_angle: float32 [8, 32], P('tomo', 'tilt'), may hold values from -1.05 to 1.05
- defocus: float32 [8, 32], P('tomo', 'tilt'), may hold values from 1 to 3
- warp: float32 [8, 32, 6], P('tomo', 'tilt'), may hold values from -0.1 to 0.1
- centers: float32 [3, 2048], replicated, may hold values from -20 to 20
- amplitudes: float32 [2048], replicated, may hold values from 0.01 to 0.05
- widths: float32 [2048], replicated, may hold values from 1 to 2.5
Outputs:
- template_grad: float32 [5, 2048], replicated
- warp_grad: float32 [8, 32, 6], P('tomo', 'tilt')
The draws below stay inside these ranges and needn't reach their ends.
Inputs may be any that keep to these rules, and one draw needn't show every extreme that they name: `anchors`: every patch of 64 x 64 pixels lies inside its tilt image.
All inputs are finite; a program needn't handle non-finite values.
Results may differ from the reference program's by a relative error of at most 0.0005.
Values may be sent and summed in bfloat16 or wider, within the bound.
No kernel may reach another device: no remote copies, remote signals or barrier semaphores. Data moves between devices by JAX's collectives and lax.ppermute only.
A program may use at most 64 MiB of HBM per device.

```python
import math
import jax
import jax.numpy as jnp
from jax import lax

G = 2048
BOX = 64
IMG = 1024
NTOMO = 8
NT = 32
P_SIZE = 32


def touch_ends(values, key, least, top_value):
    spot = [jax.random.randint(jax.random.fold_in(key, axis), (), 0, length) for axis, length in enumerate(values.shape)]
    main_axis = values.shape.index(max(values.shape))
    neighbour = spot[:main_axis] + [(spot[main_axis] + 1) % values.shape[main_axis]] + spot[main_axis + 1:]
    return values.at[tuple(spot)].set(least).at[tuple(neighbour)].set(top_value)


def levels(own_key, shape, cuts, low, largest):
    loudness = 1.0
    for dim, blocks in cuts:
        steps = jax.random.uniform(jax.random.fold_in(jax.random.fold_in(own_key, 6), dim), (blocks,), jnp.float32, low / len(cuts), largest / len(cuts))
        loudness = loudness * jnp.repeat(jnp.exp(steps), shape[dim] // blocks).reshape((-1,) + (1,) * (len(shape) - 1 - dim))
    return loudness


def noise(key, extent, width, bound, cuts=(), kind=jnp.bfloat16):
    result = width * jax.random.normal(key, extent, jnp.float32)
    if cuts:
        result = result * levels(key, extent, cuts, -0.22, 0.18)
    return jnp.clip(result, -bound, bound).astype(kind)


def setup_inputs(seed: int = 0) -> dict:
    key_of = jax.random.split(jax.random.key(seed), 10)
    return {
        "tilt_images": noise(key_of[0], (NTOMO, NT, IMG, IMG), 1.0, 6.0, ((0, 8), (1, 32))),
        "anchors": touch_ends(jax.random.randint(key_of[1], (NTOMO, NT, P_SIZE, 2), 0, IMG - BOX + 1), jax.random.fold_in(key_of[1], 1), 0, IMG - BOX).astype(jnp.int32),
        "euler": jnp.clip(jax.random.uniform(key_of[2], (NTOMO, 3, P_SIZE), jnp.float32, -3.140625, 3.140625), -3.140625, 3.140625),
        "tilt_angle": jnp.clip(jax.random.uniform(key_of[3], (NTOMO, NT), jnp.float32, -1.05, 1.05) * levels(key_of[3], (NTOMO, NT), ((0, 8), (1, 32)), -0.4, 0.0), -1.05, 1.05),
        "defocus": jnp.clip(jnp.exp(math.log(3.0) - 1.0986123 * jax.random.uniform(key_of[4], (NTOMO, NT), jnp.float32) ** levels(key_of[4], (NTOMO, NT), ((0, 8), (1, 32)), -0.2, 0.2)), 1.0, 3.0),
        "warp": jnp.clip(jax.random.uniform(key_of[5], (NTOMO, NT, 6), jnp.float32, -0.1, 0.1) * levels(key_of[5], (NTOMO, NT, 6), ((0, 8), (1, 32)), -0.4, 0.0), -0.1, 0.1),
        "centers": noise(key_of[6], (3, G), 8.0, 20.0, (), jnp.float32),
        "amplitudes": jnp.clip(jnp.exp(jax.random.uniform(key_of[7], (G,), jnp.float32, math.log(0.01), math.log(0.05))), 0.01, 0.05),
        "widths": jnp.clip(jax.random.uniform(key_of[8], (G,), jnp.float32, 1.0, 2.5), 1.0, 2.5),
    }


PRECISE = lax.Precision.HIGHEST


def signed_freqs(size_box):
    positions = jnp.arange(size_box, dtype=jnp.int32)
    return jnp.where(positions < size_box // 2, positions, positions - size_box).astype(jnp.float32)


def about_z(rotation_angle):
    c, s = jnp.cos(rotation_angle), jnp.sin(rotation_angle)
    nought = jnp.zeros_like(rotation_angle)
    unity = jnp.ones_like(rotation_angle)
    return jnp.stack([jnp.stack([c, -s, nought], -1), jnp.stack([s, c, nought], -1), jnp.stack([nought, nought, unity], -1)], -2)


def about_y(rotation_angle):
    c, s = jnp.cos(rotation_angle), jnp.sin(rotation_angle)
    nought = jnp.zeros_like(rotation_angle)
    unity = jnp.ones_like(rotation_angle)
    return jnp.stack([jnp.stack([c, nought, s], -1), jnp.stack([nought, unity, nought], -1), jnp.stack([-s, nought, c], -1)], -2)


def rotations(euler_rows, tilt_list):
    rotation = jnp.einsum("nab,nbc,ncd,nde->nae", about_y(tilt_list), about_z(euler_rows[0]), about_y(euler_rows[1]), about_z(euler_rows[2]), precision=PRECISE)
    return rotation[:, :2, :]


def ctf_table(focus_list, frequency):
    radius = frequency[:, None] ** 2 + frequency[None, :] ** 2
    return -jnp.sin(focus_list[:, None, None] * radius[None] / frequency.shape[0] + 0.1)


def slice_terms(spectrum, weight, projection, transfer, warp_row, centers, amplitudes, widths, frequency, loss_scale):
    edge = frequency.shape[0]
    phase_unit = 2.0 * math.pi / edge
    blur_unit = 2.0 * math.pi ** 2 / edge ** 2
    planar = jnp.dot(projection, centers, precision=PRECISE)
    affine = jnp.eye(2, dtype=jnp.float32) + warp_row[:4].reshape(2, 2)
    placed = jnp.dot(affine, planar, precision=PRECISE) + 20.0 * warp_row[4:6][:, None] + edge / 2
    freq_col = frequency[:, None]
    envelope = jnp.exp(-blur_unit * widths[None, :] ** 2 * freq_col ** 2)
    phase_x = phase_unit * freq_col * placed[0][None, :]
    phase_y = phase_unit * freq_col * placed[1][None, :]
    slice_xr = envelope * jnp.cos(phase_x)
    slice_xi = -envelope * jnp.sin(phase_x)
    slice_yr = amplitudes[None, :] * envelope * jnp.cos(phase_y)
    slice_yi = -amplitudes[None, :] * envelope * jnp.sin(phase_y)
    stack_x = jnp.concatenate([slice_xr, slice_xi], 0).astype(jnp.bfloat16)
    stack_y = jnp.concatenate([slice_yr, slice_yi], 0).astype(jnp.bfloat16)
    blocks = jnp.dot(stack_x, stack_y.T, preferred_element_type=jnp.float32)
    model_re = blocks[:edge, :edge] - blocks[edge:, edge:]
    model_im = blocks[:edge, edge:] + blocks[edge:, :edge]
    factor = -2.0 * loss_scale * weight * transfer
    grad_re = (factor * (spectrum[:, :edge] - transfer * model_re)).astype(jnp.bfloat16)
    grad_im = (factor * (spectrum[:, edge:] - transfer * model_im)).astype(jnp.bfloat16)
    grad_stack = jnp.concatenate([jnp.concatenate([grad_re, grad_im], 1), jnp.concatenate([grad_im, -grad_re], 1)], 0)
    back_x = jnp.dot(grad_stack, stack_y, preferred_element_type=jnp.float32)
    back_y = jnp.dot(grad_stack.T, stack_x, preferred_element_type=jnp.float32)
    back_xr, back_xi = back_x[:edge], back_x[edge:]
    back_yr, back_yi = back_y[:edge], back_y[edge:]
    move_x = phase_unit * jnp.sum(freq_col * (slice_xi * back_xr - slice_xr * back_xi), 0)
    move_y = phase_unit * jnp.sum(freq_col * (slice_yi * back_yr - slice_yr * back_yi), 0)
    inner_x = slice_xr * back_xr + slice_xi * back_xi
    inner_y = slice_yr * back_yr + slice_yi * back_yi
    curve_sum = jnp.sum(freq_col ** 2 * (inner_x + inner_y), 0)
    grad_amp = jnp.sum(inner_y, 0) / amplitudes
    grad_width = -2.0 * blur_unit * widths * curve_sum
    moves = jnp.stack([move_x, move_y])
    grad_planar = jnp.dot(affine.T, moves, precision=PRECISE)
    grad_pos = jnp.dot(projection.T, grad_planar, precision=PRECISE)
    template = jnp.concatenate([grad_pos, grad_amp[None], grad_width[None]], 0)
    warp_part = jnp.stack([jnp.sum(move_x * planar[0]), jnp.sum(move_x * planar[1]), jnp.sum(move_y * planar[0]), jnp.sum(move_y * planar[1]), 20.0 * jnp.sum(move_x), 20.0 * jnp.sum(move_y)])
    return template, warp_part


def run_patches(spectra, weights, projections, transfers, warp_rows, centers, amplitudes, widths, frequency, loss_scale):
    patch_count = spectra.shape[0]
    block_count = patch_count // 4

    def regroup(array):
        return array.reshape((block_count, 4) + array.shape[1:])

    stacked = (regroup(spectra), regroup(weights), regroup(projections), regroup(transfers), regroup(warp_rows))

    def block_step(running, pieces):
        template, warp_part = jax.vmap(lambda d, w, p, c, r: slice_terms(d, w, p, c, r, centers, amplitudes, widths, frequency, loss_scale))(*pieces)
        return running + jnp.sum(template, 0), warp_part

    running, warp_terms = lax.scan(block_step, jnp.zeros((5, centers.shape[1]), jnp.float32), stacked)
    return running, warp_terms.reshape(patch_count, 6)


def reference(tilt_images, anchors, euler, tilt_angle, defocus, warp, centers, amplitudes, widths):
    frequency = signed_freqs(BOX)
    loss_scale = 1.0 / (P_SIZE * NT)

    def one_tomogram(tomogram):
        images = tilt_images[tomogram]
        corners = anchors[tomogram]

        def cut_image(tilt_image, corner_list):
            return jax.vmap(lambda corner: lax.dynamic_slice(tilt_image, (corner[0], corner[1]), (BOX, BOX)))(corner_list)

        patches = jax.vmap(cut_image)(images, corners)
        spectra_full = jnp.fft.fft2(patches.astype(jnp.float32)) / BOX
        spectra = jnp.concatenate([spectra_full.real, spectra_full.imag], -1).astype(jnp.float32)
        power_mean = jnp.sum(spectra[..., :BOX] ** 2 + spectra[..., BOX:] ** 2, 0) / NT
        weight = 1.0 / (0.25 + power_mean)
        projections = rotations(jnp.tile(euler[tomogram], (1, NT)), jnp.repeat(tilt_angle[tomogram], P_SIZE))
        transfers = ctf_table(jnp.repeat(defocus[tomogram], P_SIZE), frequency)
        warp_rows = jnp.repeat(warp[tomogram], P_SIZE, axis=0)
        template, warp_terms = run_patches(spectra.reshape(NT * P_SIZE, BOX, 2 * BOX), jnp.tile(weight, (NT, 1, 1)), projections, transfers, warp_rows, centers, amplitudes, widths, frequency, loss_scale)
        return template, jnp.sum(warp_terms.reshape(NT, P_SIZE, 6), 1)

    templates, warps = lax.map(one_tomogram, jnp.arange(NTOMO, dtype=jnp.int32))
    return jnp.sum(templates, 0), warps
```

```python
import math

import jax
import jax.numpy as jnp
import numpy as np
from jax import lax
from jax.experimental import pallas as pl
from jax.experimental.pallas import tpu as pltpu
from jax.sharding import PartitionSpec as P

G = 2048
BOX = 64
IMG = 1024
NT = 32
NP = 32
CH = 256
NCH = G // CH
HALF = 40
ROWS = 2 * HALF
F32 = jnp.float32
BF16 = jnp.bfloat16


def _fit(fn, degree):
    n = 64
    nodes = 0.125 * (1 + np.cos(np.pi * (np.arange(n) + 0.5) / n))
    return [float(c) for c in np.polynomial.polynomial.polyfit(nodes, fn(np.sqrt(nodes)), degree)]


SIN_POLY = _fit(lambda u: np.sin(np.pi * u) / u, 5)
COS_POLY = _fit(lambda u: np.cos(np.pi * u), 5)


def _horner(w, coefs):
    acc = jnp.full_like(w, coefs[-1])
    for c in coefs[-2::-1]:
        acc = acc * w + c
    return acc


def cos_sin_turns(turns):
    u = turns - jnp.round(turns)
    w = u * u
    s = u * _horner(w, SIN_POLY)
    c = _horner(w, COS_POLY)
    return 1.0 - 2.0 * (s * s), 2.0 * (s * c)


def split(x):
    hi = x.astype(BF16)
    return hi, (x - hi.astype(F32)).astype(BF16)


def np_split(x):
    hi = x.astype(jnp.bfloat16)
    lo = (x - hi.astype(np.float64)).astype(jnp.bfloat16)
    return hi, lo


def tables():
    pos = np.arange(BOX)
    freq = np.arange(33)
    ang = 2 * np.pi * ((pos[:, None] * freq[None, :]) % BOX) / BOX
    lanes = np.zeros((BOX, 128))
    lanes[:, :33] = np.cos(ang)
    lanes[:, 64:97] = np.sin(ang)
    right = np.zeros((128, 256))
    right[:64, :128] = lanes
    right[64:, 128:] = lanes
    right_hi, right_lo = np_split(right)
    rows = np.zeros((ROWS, BOX))
    rows[:33] = np.cos(ang).T / BOX
    rows[HALF : HALF + 33] = np.sin(ang).T / BOX
    left_hi, left_lo = np_split(rows)
    left = np.concatenate([left_hi, left_hi, left_lo], 1)
    phi = np.ones(33)
    phi[0] = phi[32] = 0.5
    both = -4.0 / (NT * NP) * phi[:, None] * phi[None, :]
    plus, minus = both.copy(), both.copy()
    plus[32, 32] *= 2.0
    minus[32, 32] = 0.0
    aux = np.zeros((3, HALF, 128), np.float32)
    for base in (0, 64):
        aux[0, :33, base : base + 33] = freq[:, None] ** 2 + freq[None, :] ** 2
        aux[1, :33, base : base + 33] = plus
        aux[2, :33, base : base + 33] = minus
    return right_hi, right_lo, left, aux


def cut_kernel(anchor, angle, focus, warp, image, out):
    lane = lax.broadcasted_iota(jnp.int32, (8, 128), 1)
    sub = lax.broadcasted_iota(jnp.int32, (8, 128), 0)
    values = [angle[0, 0], focus[0, 0]] + [warp[0, 0, i] for i in range(6)]
    row = jnp.zeros((8, 128), F32)
    for i, v in enumerate(values):
        row = jnp.where(lane == i, v, row)
    hi = row.astype(BF16).astype(F32)
    mid = (row - hi).astype(BF16).astype(F32)
    low = row - hi - mid
    parts = jnp.where(sub == 0, hi, jnp.where(sub == 1, mid, jnp.where(sub == 2, low, 0.0)))
    parts = parts.astype(BF16)
    col_at = lax.broadcasted_iota(jnp.int32, (256, 128), 0)
    col_of = lax.broadcasted_iota(jnp.int32, (256, 128), 1) % BOX
    row_at = lax.broadcasted_iota(jnp.int32, (BOX, 80), 1)
    row_of = lax.broadcasted_iota(jnp.int32, (BOX, 80), 0)
    left_half = lax.broadcasted_iota(jnp.int32, (32, 128), 1) < BOX

    def one(p, carry):
        r, c = anchor[0, 0, p, 0], anchor[0, 0, p, 1]
        r0 = pl.multiple_of(jnp.minimum((r // 16) * 16, IMG - 80), 16)
        c0 = pl.multiple_of(jnp.minimum((c // 128) * 128, IMG - 256), 128)
        window = image[0, 0, pl.ds(r0, 80), pl.ds(c0, 256)]
        pick_col = jnp.where(col_at == col_of + (c - c0), 1.0, 0.0).astype(BF16)
        pick_row = jnp.where(row_at == row_of + (r - r0), 1.0, 0.0).astype(BF16)
        strip = jnp.dot(window, pick_col, preferred_element_type=F32).astype(BF16)
        patch = jnp.dot(pick_row, strip, preferred_element_type=F32)
        packed = jnp.where(left_half, patch[:32], patch[32:]).astype(BF16)
        out[p] = jnp.concatenate([packed, parts], 0)
        return carry

    lax.fori_loop(0, NP, one, 0, unroll=4)


def cut(images, anchors, angle, focus, warp):
    smem = pl.BlockSpec(memory_space=pltpu.SMEM)
    vmem = pl.BlockSpec(memory_space=pltpu.VMEM)
    return pl.pallas_call(
        cut_kernel,
        out_shape=jax.ShapeDtypeStruct((NP, 40, 128), BF16),
        in_specs=[smem, smem, smem, smem, vmem],
        out_specs=vmem,
        compiler_params=pltpu.CompilerParams(vmem_limit_bytes=16 << 20),
    )(anchors, angle, focus, warp, images)


def work_kernel(
    slot,
    euler,
    received,
    centers,
    amplitudes,
    widths,
    right_hi,
    right_lo,
    left,
    aux,
    out,
    xs,
    base,
    step,
    nyq,
    nyqk,
    env,
    acc,
    model,
    spectra,
    mats,
    zsc,
):
    prm = jnp.sum(received[:, 32:40, :].astype(F32), axis=1)
    ct, st = cos_sin_turns(prm * (0.5 / math.pi))
    ct, st = ct[:, 0:1], st[:, 0:1]
    a00, a01 = 1.0 + prm[:, 2:3], prm[:, 3:4]
    a10, a11 = prm[:, 4:5], 1.0 + prm[:, 5:6]
    sh_x, sh_y = 20.0 * prm[:, 6:7], 20.0 * prm[:, 7:8]
    mine = slot[0]
    turn = []
    for i in range(3):
        angle = jnp.full((8, 128), euler[0, i, mine], F32)
        c, s = cos_sin_turns(angle * (0.5 / math.pi))
        turn.append((c[0:1, 0:1], s[0:1, 0:1]))
    (ca, sa), (cb, sb), (cc, sc) = turn

    def rotated(sl):
        x, y, z = centers[0:1, sl], centers[1:2, sl], centers[2:3, sl]
        x, y = cc * x - sc * y, sc * x + cc * y
        x, z = cb * x + sb * z, cb * z - sb * x
        x, y = ca * x - sa * y, sa * x + ca * y
        return x, y, z

    blur = 2.0 * math.pi**2 / BOX**2
    freq8 = lax.broadcasted_iota(jnp.int32, (8, CH), 0).astype(F32)
    freq32 = lax.broadcasted_iota(jnp.int32, (32, CH), 0).astype(F32)
    first = lax.broadcasted_iota(jnp.int32, (8, CH), 0) == 0

    def prepare(c, carry):
        sl = pl.ds(pl.multiple_of(c * CH, CH), CH)
        r0, r1, r2 = rotated(sl)
        px = ct * r0 + st * r2
        ux = (a00 * px + a01 * r1 + sh_x) * (1.0 / BOX) + 0.5
        uy = (a10 * px + a11 * r1 + sh_y) * (1.0 / BOX) + 0.5
        wide = -blur * widths[0:1, sl] * widths[0:1, sl]
        damp = jnp.exp(wide * (freq32 * freq32))
        env[0, :, sl] = damp
        env[1, :, sl] = amplitudes[0:1, sl] * damp
        damp32 = jnp.exp(wide * 1024.0)
        for axis, u in ((0, ux), (1, uy)):
            u = u - jnp.round(u)
            c1, s1 = cos_sin_turns(u)
            c8, s8 = cos_sin_turns(8.0 * u)
            cn, sn = cos_sin_turns(32.0 * u)
            d32 = damp32 if axis == 0 else amplitudes[0:1, sl] * damp32
            nyq[2 * axis, :, sl] = cn * d32
            nyq[2 * axis + 1, :, sl] = sn * d32
            step[2 * axis, :, sl] = c8
            step[2 * axis + 1, :, sl] = s8

            def times(p, q):
                return p[0] * q[0] - p[1] * q[1], p[0] * q[1] + p[1] * q[0]

            e1 = (c1, s1)
            e2 = times(e1, e1)
            e3 = times(e2, e1)
            e4 = times(e2, e2)
            e5 = times(e4, e1)
            e6 = times(e3, e3)
            e7 = times(e4, e3)
            e0 = (jnp.ones_like(c1), jnp.zeros_like(c1))
            for j, e in enumerate((e0, e1, e2, e3, e4, e5, e6, e7)):
                for i in range(CH // 128):
                    tile = c * (CH // 128) + i
                    lanes = slice(i * 128, i * 128 + 128)
                    base[2 * axis, tile, pl.ds(j, NT, stride=8), :] = e[0][:, lanes]
                    base[2 * axis + 1, tile, pl.ds(j, NT, stride=8), :] = e[1][:, lanes]
        return carry

    lax.fori_loop(0, NCH, prepare, 0)

    def stacked(groups_c, groups_s, k, axis, sl):
        cn = jnp.where(first, nyq[2 * axis, pl.ds(k, 1), sl], 0.0)
        sn = jnp.where(first, nyq[2 * axis + 1, pl.ds(k, 1), sl], 0.0)
        return jnp.concatenate(groups_c + [cn] + groups_s + [sn], 0).astype(BF16)

    def forward(k, carry):
        k8 = pl.multiple_of(k * 8, 8)
        total = jnp.zeros((ROWS, ROWS), F32)
        for c in range(NCH):
            sl = slice(c * CH, (c + 1) * CH)
            sides = []
            for axis in (0, 1):
                tiles = range(c * (CH // 128), (c + 1) * (CH // 128))
                gc = jnp.concatenate([base[2 * axis, t, pl.ds(k8, 8), :] for t in tiles], 1)
                gs = jnp.concatenate([base[2 * axis + 1, t, pl.ds(k8, 8), :] for t in tiles], 1)
                rc = step[2 * axis, pl.ds(k, 1), sl]
                rs = step[2 * axis + 1, pl.ds(k, 1), sl]
                cs, ss = [], []
                for m in range(4):
                    damp = env[axis, 8 * m : 8 * m + 8, sl]
                    cm, sm = damp * gc, damp * gs
                    xs[k, axis * 64 + 8 * m : axis * 64 + 8 * m + 8, sl] = cm
                    xs[k, axis * 64 + 32 + 8 * m : axis * 64 + 40 + 8 * m, sl] = sm
                    cs.append(cm)
                    ss.append(sm)
                    if m < 3:
                        gc, gs = gc * rc - gs * rs, gc * rs + gs * rc
                sides.append(stacked(cs, ss, k, axis, sl))
            total = total + lax.dot_general(
                sides[0], sides[1], (((1,), (1,)), ((), ())), preferred_element_type=F32
            )
        model[k, :, 0:ROWS] = total
        return carry

    lax.fori_loop(0, NT, forward, 0)

    for b in range(4):
        rows = received[8 * b : 8 * b + 8, 0:32, :].reshape(256, 128)
        zsc[256 * b : 256 * b + 256, :] = jnp.dot(
            rows, right_hi[...], preferred_element_type=F32
        ) + jnp.dot(rows, right_lo[...], preferred_element_type=F32)

    lane = lax.broadcasted_iota(jnp.int32, (HALF, 128), 1)
    sign = jnp.where(lane < 64, 1.0, -1.0)

    def swap(x):
        return pltpu.roll(x, 64, 1)

    def spectrum(k, sums):
        z = zsc[pl.ds(pl.multiple_of(k * 32, 32), 32), :]
        z = jnp.concatenate([z[:, :128], z[:, 128:]], 0)
        z_hi, z_lo = split(z)
        p = jnp.dot(left[...], jnp.concatenate([z_hi, z_lo, z_hi], 0), preferred_element_type=F32)
        pc, ps = p[:HALF], swap(p[HALF:])
        spectra[k, :HALF] = pc
        spectra[k, HALF:] = ps
        plus, minus = sign * pc - ps, pc + sign * ps
        return sums[0] + plus * plus, sums[1] + minus * minus

    nought = jnp.zeros((HALF, 128), F32)
    plus, minus = lax.fori_loop(0, NT, spectrum, (nought, nought), unroll=2)
    f_plus = aux[1] / (0.25 + (plus + swap(plus)) * (1.0 / NT))
    f_minus = aux[2] / (0.25 + (minus + swap(minus)) * (1.0 / NT))
    radius = aux[0]

    def spread(x):
        return jnp.where(lane < HALF, x, pltpu.roll(x, 24, 1))

    def gather(x):
        return jnp.where(lane < HALF, x, pltpu.roll(x, 104, 1))

    lane_r = lax.broadcasted_iota(jnp.int32, (ROWS, 128), 1)

    def joined(first_part, second_part):
        moved = pltpu.roll(second_part, ROWS, 1)
        return jnp.where(lane_r < ROWS, first_part, moved), jnp.where(lane_r < 32, moved, 0.0)

    def flipped(x):
        square = jnp.concatenate([x, jnp.zeros((128 - ROWS, 128), F32)], 0)
        return jnp.transpose(square)[:ROWS]

    model[:, :, ROWS:128] = jnp.zeros((NT, ROWS, 128 - ROWS), F32)

    def residual(k, carry):
        focus = jnp.sum(received[k, 32:40, 0:128].astype(F32), axis=0, keepdims=True)[:, 1:2]
        x = focus * radius * (1.0 / BOX) + 0.1
        n = jnp.round(x * (0.5 / math.pi))
        r = (x - n * 6.28125) - n * (2.0 * math.pi - 6.28125)
        ctf = -cos_sin_turns(r * (0.5 / math.pi))[1]
        tc = spread(model[k, :HALF])
        ts = swap(spread(model[k, HALF:]))
        dc = spectra[k, :HALF] - ctf * tc
        ds = spectra[k, HALF:] - ctf * ts
        hp = (f_plus * ctf) * (sign * dc - ds)
        hm = (f_minus * ctf) * (dc + sign * ds)
        m1 = jnp.concatenate([gather(hm), gather(swap(sign * hm))], 0)
        m2 = jnp.concatenate([gather(sign * hp), gather(-swap(hp))], 0)
        for i, (u, v) in enumerate(((m1, m2), (flipped(m1), flipped(m2)))):
            lo, hi = joined(u, v)
            mats[k, i, :, 0:128] = lo.astype(BF16)
            mats[k, i, :, 128:256] = hi.astype(BF16)
        return carry

    lax.fori_loop(0, NT, residual, 0)

    acc[...] = jnp.zeros_like(acc)
    w1 = [freq8 + float(8 * m) for m in range(4)]
    w2 = [w * w for w in w1]

    def backward(k, carry):
        k8 = pl.multiple_of(k * 8, 8)
        for c in range(NCH):
            sl = slice(c * CH, (c + 1) * CH)
            sides, parts = [], []
            for axis in (0, 1):
                cs = [xs[k, axis * 64 + 8 * m : axis * 64 + 8 * m + 8, sl] for m in range(4)]
                ss = [xs[k, axis * 64 + 32 + 8 * m : axis * 64 + 40 + 8 * m, sl] for m in range(4)]
                parts.append((cs, ss))
                sides.append(stacked(cs, ss, k, axis, sl))
            width_sum = acc[0, :, sl]
            for axis in (0, 1):
                other = sides[1 - axis]
                back = jnp.dot(
                    mats[k, axis, :, 0 : 2 * ROWS],
                    jnp.concatenate([other, other], 0),
                    preferred_element_type=F32,
                )
                cs, ss = parts[axis]
                move, value = None, None
                for m in range(4):
                    kc = back[8 * m : 8 * m + 8]
                    ks = back[HALF + 8 * m : HALF + 8 * m + 8]
                    re = cs[m] * kc + ss[m] * ks
                    im = cs[m] * ks - ss[m] * kc
                    width_sum = width_sum + w2[m] * re
                    move = w1[m] * im if move is None else move + w1[m] * im
                    value = re if value is None else value + re
                if axis == 1:
                    acc[1, :, sl] = acc[1, :, sl] + value
                for i in range(CH // 128):
                    base[axis, c * (CH // 128) + i, pl.ds(k8, 8), :] = move[:, i * 128 : i * 128 + 128]
                nyqk[2 * axis, pl.ds(k, 1), sl] = back[32:33]
                nyqk[2 * axis + 1, pl.ds(k, 1), sl] = back[HALF + 32 : HALF + 33]
            acc[0, :, sl] = width_sum
        return carry

    lax.fori_loop(0, NT, backward, 0)

    terms = [jnp.zeros((NT, 128), F32) for _ in range(6)]
    unit = 2.0 * math.pi / BOX
    for c in range(G // 128):
        sl = slice(c * 128, (c + 1) * 128)
        moves, ends = [], []
        for axis in (0, 1):
            move = base[axis, c, pl.ds(0, NT, stride=8), :]
            for j in range(1, 8):
                move = move + base[axis, c, pl.ds(j, NT, stride=8), :]
            nc, ns = nyq[2 * axis, :, sl], nyq[2 * axis + 1, :, sl]
            kc, ks = nyqk[2 * axis, :, sl], nyqk[2 * axis + 1, :, sl]
            moves.append(unit * (move + 32.0 * (nc * ks - ns * kc)))
            ends.append(jnp.sum(nc * kc + ns * ks, axis=0, keepdims=True))
        mx, my = moves
        r0, r1, r2 = rotated(sl)
        px = ct * r0 + st * r2
        for i, t in enumerate((mx * px, mx * r1, my * px, my * r1, mx, my)):
            terms[i] = terms[i] + t
        vx = a00 * mx + a10 * my
        vy = a01 * mx + a11 * my
        x = jnp.sum(ct * vx, axis=0, keepdims=True)
        z = jnp.sum(st * vx, axis=0, keepdims=True)
        y = jnp.sum(vy, axis=0, keepdims=True)
        x, y = ca * x + sa * y, ca * y - sa * x
        x, z = cb * x - sb * z, sb * x + cb * z
        x, y = cc * x + sc * y, cc * y - sc * x
        curve = jnp.sum(acc[0, :, sl], axis=0, keepdims=True) + 1024.0 * (ends[0] + ends[1])
        value = jnp.sum(acc[1, :, sl], axis=0, keepdims=True) + ends[1]
        out[2 * c, 0:1, :] = x
        out[2 * c, 1:2, :] = y
        out[2 * c, 2:3, :] = z
        out[2 * c + 1, 0:1, :] = value / amplitudes[0:1, sl]
        out[2 * c + 1, 1:2, :] = (-2.0 * blur) * widths[0:1, sl] * curve
        out[2 * c + 1, 2:3, :] = jnp.zeros((1, 128), F32)
    lane_w = lax.broadcasted_iota(jnp.int32, (NT, 128), 1)
    warp_rows = jnp.zeros((NT, 128), F32)
    for i in range(6):
        total = jnp.sum(terms[i], axis=1, keepdims=True) * (20.0 if i > 3 else 1.0)
        warp_rows = jnp.where(lane_w == i, total, warp_rows)
    for k in range(NT):
        out[k, 3:4, :] = warp_rows[k : k + 1]


def work(slot, euler, received, centers, amplitudes, widths):
    smem = pl.BlockSpec(memory_space=pltpu.SMEM)
    vmem = pl.BlockSpec(memory_space=pltpu.VMEM)
    right_hi, right_lo, left, aux = tables()
    return pl.pallas_call(
        work_kernel,
        out_shape=jax.ShapeDtypeStruct((NT, 4, 128), F32),
        in_specs=[smem, smem] + [vmem] * 8,
        out_specs=vmem,
        scratch_shapes=[
            pltpu.VMEM((NT, 128, G), F32),
            pltpu.VMEM((4, G // 128, NT * 8, 128), F32),
            pltpu.VMEM((4, NT, G), F32),
            pltpu.VMEM((4, NT, G), F32),
            pltpu.VMEM((4, NT, G), F32),
            pltpu.VMEM((2, 32, G), F32),
            pltpu.VMEM((2, 8, G), F32),
            pltpu.VMEM((NT, ROWS, 128), F32),
            pltpu.VMEM((NT, ROWS, 128), F32),
            pltpu.VMEM((NT, 2, ROWS, 256), BF16),
            pltpu.VMEM((1024, 256), F32),
        ],
        compiler_params=pltpu.CompilerParams(vmem_limit_bytes=60 << 20),
    )(
        slot,
        euler,
        received,
        centers,
        amplitudes.reshape(1, G),
        widths.reshape(1, G),
        jnp.asarray(right_hi),
        jnp.asarray(right_lo),
        jnp.asarray(left),
        jnp.asarray(aux),
    )


def on_device(tilt_images, anchors, euler, tilt_angle, defocus, warp, centers, amplitudes, widths):
    payload = cut(tilt_images, anchors, tilt_angle, defocus, warp)
    received = lax.all_to_all(payload, "tilt", split_axis=0, concat_axis=0, tiled=True)
    slot = lax.axis_index("tilt").astype(jnp.int32).reshape(1)
    partial = work(slot, euler, received, centers, amplitudes, widths)
    shares = lax.all_to_all(partial, "tilt", split_axis=0, concat_axis=0, tiled=True)
    own = jnp.sum(shares, 0)
    warp_local = own[3, :6]
    tomos = lax.all_to_all(
        jnp.broadcast_to(own[None], (8, 4, 128)), "tomo", split_axis=0, concat_axis=0, tiled=True
    )
    chunk = jnp.sum(tomos, 0)
    whole = lax.all_to_all(
        jnp.broadcast_to(chunk[None], (NT, 4, 128)), "tilt", split_axis=0, concat_axis=0, tiled=True
    )
    whole = whole.reshape(16, 2, 4, 128)
    rows = jnp.concatenate([whole[:, 0, 0:3], whole[:, 1, 0:2]], 1)
    template = jnp.transpose(rows, (1, 0, 2)).reshape(5, G)
    return (template, warp_local.reshape(1, 1, 6))


def solution(mesh):
    placed = (
        P("tomo", "tilt", None, None),
        P("tomo", "tilt", None, None),
        P("tomo", None, None),
        P("tomo", "tilt"),
        P("tomo", "tilt"),
        P("tomo", "tilt", None),
        P(),
        P(),
        P(),
    )
    return jax.shard_map(
        on_device,
        mesh=mesh,
        in_specs=placed,
        out_specs=(P(), P("tomo", "tilt", None)),
        check_vma=False,
    )
```

```python
import math

import jax
import jax.numpy as jnp
import numpy as np
from jax import lax
from jax.experimental import pallas as pl
from jax.experimental.pallas import tpu as pltpu
from jax.sharding import PartitionSpec as P

G = 2048
BOX = 64
IMG = 1024
NT = 32
NP = 32
CH = 256
NCH = G // CH
HALF = 40
ROWS = 2 * HALF
UF, US, UR, UB = 2, 8, 8, 2
F32 = jnp.float32
BF16 = jnp.bfloat16


def _fit(fn, degree):
    n = 64
    nodes = 0.125 * (1 + np.cos(np.pi * (np.arange(n) + 0.5) / n))
    return [float(c) for c in np.polynomial.polynomial.polyfit(nodes, fn(np.sqrt(nodes)), degree)]


SIN_POLY = _fit(lambda u: np.sin(np.pi * u) / u, 5)
COS_POLY = _fit(lambda u: np.cos(np.pi * u), 5)


def _horner(w, coefs):
    acc = jnp.full_like(w, coefs[-1])
    for c in coefs[-2::-1]:
        acc = acc * w + c
    return acc


def cos_sin_turns(turns):
    u = turns - jnp.round(turns)
    w = u * u
    s = u * _horner(w, SIN_POLY)
    c = _horner(w, COS_POLY)
    return 1.0 - 2.0 * (s * s), 2.0 * (s * c)


def split(x):
    hi = x.astype(BF16)
    return hi, (x - hi.astype(F32)).astype(BF16)


def np_split(x):
    hi = x.astype(jnp.bfloat16)
    lo = (x - hi.astype(np.float64)).astype(jnp.bfloat16)
    return hi, lo


def tables():
    pos = np.arange(BOX)
    freq = np.arange(33)
    ang = 2 * np.pi * ((pos[:, None] * freq[None, :]) % BOX) / BOX
    lanes = np.zeros((BOX, 128))
    lanes[:, :33] = np.cos(ang)
    lanes[:, 64:97] = np.sin(ang)
    right = np.zeros((128, 256))
    right[:64, :128] = lanes
    right[64:, 128:] = lanes
    right_hi, right_lo = np_split(right)
    rows = np.zeros((ROWS, BOX))
    rows[:33] = np.cos(ang).T / BOX
    rows[HALF : HALF + 33] = np.sin(ang).T / BOX
    left_hi, left_lo = np_split(rows)
    left = np.concatenate([left_hi, left_hi, left_lo], 1)
    phi = np.ones(33)
    phi[0] = phi[32] = 0.5
    both = -4.0 / (NT * NP) * phi[:, None] * phi[None, :]
    plus, minus = both.copy(), both.copy()
    plus[32, 32] *= 2.0
    minus[32, 32] = 0.0
    aux = np.zeros((3, HALF, 128), np.float32)
    for base in (0, 64):
        aux[0, :33, base : base + 33] = freq[:, None] ** 2 + freq[None, :] ** 2
        aux[1, :33, base : base + 33] = plus
        aux[2, :33, base : base + 33] = minus
    joiner = np.zeros((256, 2 * ROWS), jnp.bfloat16)
    chooser = np.zeros((ROWS, 128), jnp.bfloat16)
    for i in range(HALF):
        for part in (0, 1):
            joiner[128 * part + i, ROWS * part + i] = 1
            joiner[128 * part + 64 + i, ROWS * part + HALF + i] = 1
        chooser[i, i] = 1
        chooser[HALF + i, 64 + i] = 1
    return right_hi, right_lo, left, joiner, chooser, aux


def cut_kernel(anchor, angle, focus, warp, image, out, windows, sem, strip):
    def source(p):
        r, c = anchor[0, 0, 0, p], anchor[0, 0, 1, p]
        r0 = pl.multiple_of(jnp.minimum((r // 16) * 16, IMG - 80), 16)
        c0 = pl.multiple_of(jnp.minimum((c // 128) * 128, IMG - 256), 128)
        return r, c, r0, c0

    def copy(p):
        _, _, r0, c0 = source(p)
        return pltpu.make_async_copy(
            image.at[0, 0, pl.ds(r0, 80), pl.ds(c0, 256)], windows.at[p], sem.at[p]
        )

    def start(p, carry):
        copy(p).start()
        return carry

    lax.fori_loop(0, NP, start, 0, unroll=4)

    lane = lax.broadcasted_iota(jnp.int32, (8, 128), 1)
    sub = lax.broadcasted_iota(jnp.int32, (8, 128), 0)
    values = [angle[0, 0], focus[0, 0]] + [warp[0, 0, i] for i in range(6)]
    row = jnp.zeros((8, 128), F32)
    for i, v in enumerate(values):
        row = jnp.where(lane == i, v, row)
    hi = row.astype(BF16).astype(F32)
    mid = (row - hi).astype(BF16).astype(F32)
    low = row - hi - mid
    parts = jnp.where(sub == 0, hi, jnp.where(sub == 1, mid, jnp.where(sub == 2, low, 0.0)))
    left_half = lax.broadcasted_iota(jnp.int32, (32, 128), 1) < BOX

    def one(p, carry):
        copy(p).wait()
        r, c, r0, c0 = source(p)
        turned = pltpu.roll(windows[p].astype(F32), 256 - (c - c0), 1)[:, :128]
        strip[p % 8] = turned
        upper = strip[p % 8, pl.ds(r - r0, 32), :]
        lower = strip[p % 8, pl.ds(r - r0 + 32, 32), :]
        packed = jnp.where(left_half, upper, pltpu.roll(lower, 64, 1))
        out[p] = jnp.concatenate([packed, parts], 0).astype(BF16)
        return carry

    lax.fori_loop(0, NP, one, 0, unroll=8)


def cut(images, anchors, angle, focus, warp):
    smem = pl.BlockSpec(memory_space=pltpu.SMEM)
    return pl.pallas_call(
        cut_kernel,
        out_shape=jax.ShapeDtypeStruct((NP, 40, 128), BF16),
        in_specs=[smem, smem, smem, smem, pl.BlockSpec(memory_space=pl.ANY)],
        out_specs=pl.BlockSpec(memory_space=pltpu.VMEM),
        scratch_shapes=[
            pltpu.VMEM((NP, 80, 256), BF16),
            pltpu.SemaphoreType.DMA((NP,)),
            pltpu.VMEM((8, 80, 128), F32),
        ],
        compiler_params=pltpu.CompilerParams(vmem_limit_bytes=55 << 20),
    )(jnp.transpose(anchors, (0, 1, 3, 2)), angle, focus, warp, images)


def work_kernel(
    slot,
    euler,
    received,
    centers,
    amplitudes,
    widths,
    right_hi,
    right_lo,
    left,
    joiner,
    chooser,
    aux,
    keep,
    send,
    xs,
    base,
    step,
    nyq,
    nyqk,
    env,
    acc,
    model,
    spectra,
    mats,
    zsc,
    focus,
    out,
):
    prm = jnp.sum(received[:, 32:40, :].astype(F32), axis=1)
    focus[...] = jnp.broadcast_to(prm[:, 1:2], (NT, 128))
    ct, st = cos_sin_turns(prm * (0.5 / math.pi))
    ct, st = ct[:, 0:1], st[:, 0:1]
    a00, a01 = 1.0 + prm[:, 2:3], prm[:, 3:4]
    a10, a11 = prm[:, 4:5], 1.0 + prm[:, 5:6]
    sh_x, sh_y = 20.0 * prm[:, 6:7], 20.0 * prm[:, 7:8]
    mine = slot[0]
    turn = []
    for i in range(3):
        angle = jnp.full((8, 128), euler[i, 0, mine], F32)
        c, s = cos_sin_turns(angle * (0.5 / math.pi))
        turn.append((c[0:1, 0:1], s[0:1, 0:1]))
    (ca, sa), (cb, sb), (cc, sc) = turn

    def rotated(sl):
        x, y, z = centers[0:1, sl], centers[1:2, sl], centers[2:3, sl]
        x, y = cc * x - sc * y, sc * x + cc * y
        x, z = cb * x + sb * z, cb * z - sb * x
        x, y = ca * x - sa * y, sa * x + ca * y
        return x, y, z

    blur = 2.0 * math.pi**2 / BOX**2
    freq8 = lax.broadcasted_iota(jnp.int32, (8, CH), 0).astype(F32)
    freq32 = lax.broadcasted_iota(jnp.int32, (32, CH), 0).astype(F32)
    first = lax.broadcasted_iota(jnp.int32, (8, CH), 0) == 0

    def prepare(c, carry):
        sl = pl.ds(pl.multiple_of(c * CH, CH), CH)
        r0, r1, r2 = rotated(sl)
        px = ct * r0 + st * r2
        ux = (a00 * px + a01 * r1 + sh_x) * (1.0 / BOX) + 0.5
        uy = (a10 * px + a11 * r1 + sh_y) * (1.0 / BOX) + 0.5
        wide = -blur * widths[0:1, sl] * widths[0:1, sl]
        damp = jnp.exp(wide * (freq32 * freq32))
        env[0, :, sl] = damp
        env[1, :, sl] = amplitudes[0:1, sl] * damp
        damp32 = jnp.exp(wide * 1024.0)
        for axis, u in ((0, ux), (1, uy)):
            u = u - jnp.round(u)
            c1, s1 = cos_sin_turns(u)
            def twice(p):
                return 1.0 - 2.0 * (p[1] * p[1]), 2.0 * (p[0] * p[1])

            def times(p, q):
                return p[0] * q[0] - p[1] * q[1], p[0] * q[1] + p[1] * q[0]

            e1 = (c1, s1)
            e2 = twice(e1)
            e3 = times(e2, e1)
            e4 = twice(e2)
            e5 = times(e4, e1)
            e6 = twice(e3)
            e7 = times(e4, e3)
            c8, s8 = e8 = twice(e4)
            cn, sn = twice(twice(e8))
            d32 = damp32 if axis == 0 else amplitudes[0:1, sl] * damp32
            nyq[2 * axis, :, sl] = cn * d32
            nyq[2 * axis + 1, :, sl] = sn * d32
            step[2 * axis, :, sl] = c8
            step[2 * axis + 1, :, sl] = s8
            e0 = (jnp.ones_like(c1), jnp.zeros_like(c1))
            for j, e in enumerate((e0, e1, e2, e3, e4, e5, e6, e7)):
                for i in range(CH // 128):
                    tile = c * (CH // 128) + i
                    lanes = slice(i * 128, i * 128 + 128)
                    base[2 * axis, tile, pl.ds(j, NT, stride=8), :] = e[0][:, lanes]
                    base[2 * axis + 1, tile, pl.ds(j, NT, stride=8), :] = e[1][:, lanes]
        return carry

    lax.fori_loop(0, NCH, prepare, 0)

    blank = jnp.zeros((24, CH), F32)

    def factors(k, axis, c):
        sl = slice(c * CH, (c + 1) * CH)
        k8 = pl.multiple_of(k * 8, 8)
        tiles = range(c * (CH // 128), (c + 1) * (CH // 128))
        gc = jnp.concatenate([base[2 * axis, t, pl.ds(k8, 8), :] for t in tiles], 1)
        gs = jnp.concatenate([base[2 * axis + 1, t, pl.ds(k8, 8), :] for t in tiles], 1)
        rc = step[2 * axis, pl.ds(k, 1), sl]
        rs = step[2 * axis + 1, pl.ds(k, 1), sl]
        cs, ss = [], []
        for m in range(4):
            damp = env[axis, 8 * m : 8 * m + 8, sl]
            cm, sm = damp * gc, damp * gs
            xs[k, axis * 64 + 8 * m : axis * 64 + 8 * m + 8, sl] = cm
            xs[k, axis * 64 + 32 + 8 * m : axis * 64 + 40 + 8 * m, sl] = sm
            cs.append(cm)
            ss.append(sm)
            if m < 3:
                gc, gs = gc * rc - gs * rs, gc * rs + gs * rc
        return cs, ss

    def ends_of(k, axis, sl):
        cn = jnp.where(first, nyq[2 * axis, pl.ds(k, 1), sl], 0.0)
        sn = jnp.where(first, nyq[2 * axis + 1, pl.ds(k, 1), sl], 0.0)
        return [cn], [sn]

    def forward(b, carry):
        total = jnp.zeros((2 * ROWS, 256), F32)
        for c in range(NCH):
            sl = slice(c * CH, (c + 1) * CH)
            left_rows, right_rows = [], []
            for k in (2 * b, 2 * b + 1):
                cs, ss = factors(k, 0, c)
                cn, sn = ends_of(k, 0, sl)
                left_rows += cs + cn + ss + sn
                cs, ss = factors(k, 1, c)
                cn, sn = ends_of(k, 1, sl)
                right_rows += cs + cn + [blank] + ss + sn + [blank]
            total = total + lax.dot_general(
                jnp.concatenate(left_rows, 0).astype(BF16),
                jnp.concatenate(right_rows, 0).astype(BF16),
                (((1,), (1,)), ((), ())),
                preferred_element_type=F32,
            )
        model[2 * b] = total[:ROWS, :128]
        model[2 * b + 1] = total[ROWS:, 128:]
        return carry

    lax.fori_loop(0, NT // 2, forward, 0, unroll=UF)

    for b in range(4):
        rows = received[8 * b : 8 * b + 8, 0:32, :].reshape(256, 128)
        zsc[256 * b : 256 * b + 256, :] = jnp.dot(
            rows, right_hi[...], preferred_element_type=F32
        ) + jnp.dot(rows, right_lo[...], preferred_element_type=F32)

    lane = lax.broadcasted_iota(jnp.int32, (HALF, 128), 1)
    sign = jnp.where(lane < 64, 1.0, -1.0)

    def swap(x):
        return pltpu.roll(x, 64, 1)

    def spectrum(k, sums):
        z = zsc[pl.ds(pl.multiple_of(k * 32, 32), 32), :]
        z = jnp.concatenate([z[:, :128], z[:, 128:]], 0)
        z_hi, z_lo = split(z)
        p = jnp.dot(left[...], jnp.concatenate([z_hi, z_lo, z_hi], 0), preferred_element_type=F32)
        pc, ps = p[:HALF], swap(p[HALF:])
        spectra[k, :HALF] = pc
        spectra[k, HALF:] = ps
        plus, minus = sign * pc - ps, pc + sign * ps
        return sums[0] + plus * plus, sums[1] + minus * minus

    nought = jnp.zeros((HALF, 128), F32)
    plus, minus = lax.fori_loop(0, NT, spectrum, (nought, nought), unroll=US)
    f_plus = aux[1] / (0.25 + (plus + swap(plus)) * (1.0 / NT))
    f_minus = aux[2] / (0.25 + (minus + swap(minus)) * (1.0 / NT))
    radius = aux[0]

    def residual(k, carry):
        x = focus[pl.ds(k, 1), :] * radius * (1.0 / BOX) + 0.1
        n = jnp.round(x * (0.5 / math.pi))
        r = (x - n * 6.28125) - n * (2.0 * math.pi - 6.28125)
        ctf = -cos_sin_turns(r * (0.5 / math.pi))[1]
        dc = spectra[k, :HALF] - ctf * model[k, :HALF]
        ds = spectra[k, HALF:] - ctf * swap(model[k, HALF:])
        hp = (f_plus * ctf) * (sign * dc - ds)
        hm = (f_minus * ctf) * (dc + sign * ds)
        m1 = jnp.concatenate([hm, swap(sign * hm)], 0).astype(BF16)
        m2 = jnp.concatenate([sign * hp, -swap(hp)], 0).astype(BF16)
        mats[k, 0] = jnp.dot(
            jnp.concatenate([m1, m2], 1), joiner[...], preferred_element_type=F32
        ).astype(BF16)
        mats[k, 1] = lax.dot_general(
            chooser[...],
            jnp.concatenate([m1, m2], 0),
            (((1,), (1,)), ((), ())),
            preferred_element_type=F32,
        ).astype(BF16)
        return carry

    lax.fori_loop(0, NT, residual, 0, unroll=UR)

    acc[...] = jnp.zeros_like(acc)
    w1 = [freq8 + float(8 * m) for m in range(4)]
    w2 = [w * w for w in w1]

    def backward(k, carry):
        k8 = pl.multiple_of(k * 8, 8)
        for c in range(NCH):
            sl = slice(c * CH, (c + 1) * CH)
            sides, parts = [], []
            for axis in (0, 1):
                cs = [xs[k, axis * 64 + 8 * m : axis * 64 + 8 * m + 8, sl] for m in range(4)]
                ss = [xs[k, axis * 64 + 32 + 8 * m : axis * 64 + 40 + 8 * m, sl] for m in range(4)]
                cn, sn = ends_of(k, axis, sl)
                parts.append((cs, ss))
                sides.append(jnp.concatenate(cs + cn + ss + sn, 0).astype(BF16))
            backs = [
                jnp.dot(
                    mats[k, axis],
                    jnp.concatenate([sides[1 - axis]] * 2, 0),
                    preferred_element_type=F32,
                )
                for axis in (0, 1)
            ]
            width_sum = acc[0, :, sl]
            value_sum = acc[1, :, sl]
            moves = [None, None]
            for m in range(4):
                values = []
                for axis in (0, 1):
                    c_m, s_m = parts[axis][0][m], parts[axis][1][m]
                    kc = backs[axis][8 * m : 8 * m + 8]
                    ks = backs[axis][HALF + 8 * m : HALF + 8 * m + 8]
                    values.append(c_m * kc + s_m * ks)
                    move = w1[m] * (c_m * ks - s_m * kc)
                    moves[axis] = move if m == 0 else moves[axis] + move
                value_sum = value_sum + values[1]
                width_sum = width_sum + w2[m] * (values[0] + values[1])
            acc[0, :, sl] = width_sum
            acc[1, :, sl] = value_sum
            for axis in (0, 1):
                for i in range(CH // 128):
                    lanes = slice(i * 128, i * 128 + 128)
                    base[axis, c * (CH // 128) + i, pl.ds(k8, 8), :] = moves[axis][:, lanes]
                nyqk[2 * axis, pl.ds(k, 1), sl] = backs[axis][32:33]
                nyqk[2 * axis + 1, pl.ds(k, 1), sl] = backs[axis][HALF + 32 : HALF + 33]
        return carry

    lax.fori_loop(0, NT, backward, 0, unroll=UB)

    terms = [jnp.zeros((NT, 128), F32) for _ in range(6)]
    unit = 2.0 * math.pi / BOX
    for c in range(G // 128):
        sl = slice(c * 128, (c + 1) * 128)
        moves, ends = [], []
        for axis in (0, 1):
            move = base[axis, c, pl.ds(0, NT, stride=8), :]
            for j in range(1, 8):
                move = move + base[axis, c, pl.ds(j, NT, stride=8), :]
            nc, ns = nyq[2 * axis, :, sl], nyq[2 * axis + 1, :, sl]
            kc, ks = nyqk[2 * axis, :, sl], nyqk[2 * axis + 1, :, sl]
            moves.append(unit * (move + 32.0 * (nc * ks - ns * kc)))
            ends.append(jnp.sum(nc * kc + ns * ks, axis=0, keepdims=True))
        mx, my = moves
        r0, r1, r2 = rotated(sl)
        px = ct * r0 + st * r2
        for i, t in enumerate((mx * px, mx * r1, my * px, my * r1, mx, my)):
            terms[i] = terms[i] + t
        vx = a00 * mx + a10 * my
        vy = a01 * mx + a11 * my
        x = jnp.sum(ct * vx, axis=0, keepdims=True)
        z = jnp.sum(st * vx, axis=0, keepdims=True)
        y = jnp.sum(vy, axis=0, keepdims=True)
        x, y = ca * x + sa * y, ca * y - sa * x
        x, z = cb * x - sb * z, sb * x + cb * z
        x, y = cc * x + sc * y, cc * y - sc * x
        curve = jnp.sum(acc[0, :, sl], axis=0, keepdims=True) + 1024.0 * (ends[0] + ends[1])
        value = jnp.sum(acc[1, :, sl], axis=0, keepdims=True) + ends[1]
        half, lanes = c // 8, slice((c % 8) * 128, (c % 8) * 128 + 128)
        out[half, 0:1, lanes] = x
        out[half, 1:2, lanes] = y
        out[half, 2:3, lanes] = z
        out[half, 3:4, lanes] = value / amplitudes[0:1, sl]
        out[half, 4:5, lanes] = (-2.0 * blur) * widths[0:1, sl] * curve
    lane_w = lax.broadcasted_iota(jnp.int32, (NT, 128), 1)
    warp_rows = jnp.zeros((NT, 128), F32)
    for i in range(6):
        total = jnp.sum(terms[i], axis=1, keepdims=True) * (20.0 if i > 3 else 1.0)
        warp_rows = jnp.where(lane_w == i, total, warp_rows)
    for k in range(NT):
        i = k // 2
        out[k % 2, 5 + i // 8 : 6 + i // 8, (i % 8) * 128 : (i % 8) * 128 + 128] = warp_rows[k : k + 1]
    core = mine % 2
    keep[...] = out[core]
    send[...] = out[1 - core]


def work(slot, euler, received, centers, amplitudes, widths):
    smem = pl.BlockSpec(memory_space=pltpu.SMEM)
    vmem = pl.BlockSpec(memory_space=pltpu.VMEM)
    right_hi, right_lo, left, joiner, chooser, aux = tables()
    return pl.pallas_call(
        work_kernel,
        out_shape=[jax.ShapeDtypeStruct((8, G // 2), F32)] * 2,
        in_specs=[smem, smem] + [vmem] * 10,
        out_specs=[vmem, vmem],
        scratch_shapes=[
            pltpu.VMEM((NT, 128, G), F32),
            pltpu.VMEM((4, G // 128, NT * 8, 128), F32),
            pltpu.VMEM((4, NT, G), F32),
            pltpu.VMEM((4, NT, G), F32),
            pltpu.VMEM((4, NT, G), F32),
            pltpu.VMEM((2, 32, G), F32),
            pltpu.VMEM((2, 8, G), F32),
            pltpu.VMEM((NT, ROWS, 128), F32),
            pltpu.VMEM((NT, ROWS, 128), F32),
            pltpu.VMEM((NT, 2, ROWS, 2 * ROWS), BF16),
            pltpu.VMEM((1024, 256), F32),
            pltpu.VMEM((NT, 128), F32),
            pltpu.VMEM((2, 8, G // 2), F32),
        ],
        compiler_params=pltpu.CompilerParams(vmem_limit_bytes=55 << 20),
    )(
        slot,
        jnp.transpose(euler, (1, 0, 2)),
        received,
        centers,
        amplitudes.reshape(1, G),
        widths.reshape(1, G),
        jnp.asarray(right_hi),
        jnp.asarray(right_lo),
        jnp.asarray(left),
        jnp.asarray(joiner),
        jnp.asarray(chooser),
        jnp.asarray(aux),
    )


def exchanged(value, axis, mask):
    return lax.ppermute(value, axis, [(i, i ^ mask) for i in range(lax.axis_size(axis))])


def on_device(tilt_images, anchors, euler, tilt_angle, defocus, warp, centers, amplitudes, widths):
    payload = cut(tilt_images, anchors, tilt_angle, defocus, warp)
    received = lax.all_to_all(payload, "tilt", split_axis=0, concat_axis=0, tiled=True)
    index = lax.axis_index("tilt").astype(jnp.int32)
    total, other = work(index.reshape(1), euler, received, centers, amplitudes, widths)
    total = total + exchanged(other, "tilt", 1)
    for mask in (2, 6, 8, 24):
        total = total + exchanged(total, "tilt", mask)
    place = index // 2
    warp_local = lax.dynamic_slice(total, (5 + place // 8, (place % 8) * 128), (1, 6))
    for mask in (1, 2, 7):
        total = total + exchanged(total, "tomo", mask)
    other = exchanged(total, "tilt", 1)
    first = index % 2 == 0
    template = jnp.concatenate(
        [jnp.where(first, total, other)[:5], jnp.where(first, other, total)[:5]], 1
    )
    return (template, warp_local.reshape(1, 1, 6))


def solution(mesh):
    placed = (
        P("tomo", "tilt", None, None),
        P("tomo", "tilt", None, None),
        P("tomo", None, None),
        P("tomo", "tilt"),
        P("tomo", "tilt"),
        P("tomo", "tilt", None),
        P(),
        P(),
        P(),
    )
    return jax.shard_map(
        on_device,
        mesh=mesh,
        in_specs=placed,
        out_specs=(P(), P("tomo", "tilt", None)),
        check_vma=False,
    )
```

```python
import math

import jax
import jax.numpy as jnp
import numpy as np
from jax import lax
from jax.experimental import pallas as pl
from jax.experimental.pallas import tpu as pltpu
from jax.sharding import PartitionSpec as P

G = 2048
BOX = 64
IMG = 1024
NT = 32
NP = 32
CH = 256
NCH = G // CH
HALF = 40
ROWS = 2 * HALF
UF, US, UR, UB = 2, 8, 8, 2
F32 = jnp.float32
BF16 = jnp.bfloat16


def _fit(fn, degree):
    n = 64
    nodes = 0.125 * (1 + np.cos(np.pi * (np.arange(n) + 0.5) / n))
    return [float(c) for c in np.polynomial.polynomial.polyfit(nodes, fn(np.sqrt(nodes)), degree)]


SIN_POLY = _fit(lambda u: np.sin(np.pi * u) / u, 5)
COS_POLY = _fit(lambda u: np.cos(np.pi * u), 5)


def _horner(w, coefs):
    acc = jnp.full_like(w, coefs[-1])
    for c in coefs[-2::-1]:
        acc = acc * w + c
    return acc


def cos_sin_turns(turns):
    u = turns - jnp.round(turns)
    w = u * u
    s = u * _horner(w, SIN_POLY)
    c = _horner(w, COS_POLY)
    return 1.0 - 2.0 * (s * s), 2.0 * (s * c)


def split(x):
    hi = x.astype(BF16)
    return hi, (x - hi.astype(F32)).astype(BF16)


def np_split(x):
    hi = x.astype(jnp.bfloat16)
    lo = (x - hi.astype(np.float64)).astype(jnp.bfloat16)
    return hi, lo


def tables():
    pos = np.arange(BOX)
    freq = np.arange(33)
    ang = 2 * np.pi * ((pos[:, None] * freq[None, :]) % BOX) / BOX
    lanes = np.zeros((BOX, 128))
    lanes[:, :33] = np.cos(ang)
    lanes[:, 64:97] = np.sin(ang)
    right = np.zeros((128, 256))
    right[:64, :128] = lanes
    right[64:, 128:] = lanes
    right_hi, right_lo = np_split(right)
    rows = np.zeros((ROWS, BOX))
    rows[:33] = np.cos(ang).T / BOX
    rows[HALF : HALF + 33] = np.sin(ang).T / BOX
    left_hi, left_lo = np_split(rows)
    left = np.concatenate([left_hi, left_hi, left_lo], 1)
    phi = np.ones(33)
    phi[0] = phi[32] = 0.5
    both = -4.0 / (NT * NP) * phi[:, None] * phi[None, :]
    plus, minus = both.copy(), both.copy()
    plus[32, 32] *= 2.0
    minus[32, 32] = 0.0
    aux = np.zeros((3, HALF, 128), np.float32)
    for base in (0, 64):
        aux[0, :33, base : base + 33] = freq[:, None] ** 2 + freq[None, :] ** 2
        aux[1, :33, base : base + 33] = plus
        aux[2, :33, base : base + 33] = minus
    joiner = np.zeros((256, 2 * ROWS), jnp.bfloat16)
    chooser = np.zeros((ROWS, 128), jnp.bfloat16)
    for i in range(HALF):
        for part in (0, 1):
            joiner[128 * part + i, ROWS * part + i] = 1
            joiner[128 * part + 64 + i, ROWS * part + HALF + i] = 1
        chooser[i, i] = 1
        chooser[HALF + i, 64 + i] = 1
    return right_hi, right_lo, left, joiner, chooser, aux


def cut_kernel(anchor, angle, focus, warp, image, out, held, sem, strip):
    copy = pltpu.make_async_copy(image.at[0, 0], held, sem)
    copy.start()
    lane = lax.broadcasted_iota(jnp.int32, (8, 128), 1)
    sub = lax.broadcasted_iota(jnp.int32, (8, 128), 0)
    values = [angle[0, 0], focus[0, 0]] + [warp[0, 0, i] for i in range(6)]
    row = jnp.zeros((8, 128), F32)
    for i, v in enumerate(values):
        row = jnp.where(lane == i, v, row)
    hi = row.astype(BF16).astype(F32)
    mid = (row - hi).astype(BF16).astype(F32)
    low = row - hi - mid
    parts = jnp.where(sub == 0, hi, jnp.where(sub == 1, mid, jnp.where(sub == 2, low, 0.0)))
    left_half = lax.broadcasted_iota(jnp.int32, (32, 128), 1) < BOX

    copy.wait()

    def one(p, carry):
        r, c = anchor[0, 0, 0, p], anchor[0, 0, 1, p]
        r0 = pl.multiple_of(jnp.minimum((r // 16) * 16, IMG - 80), 16)
        c0 = pl.multiple_of(jnp.minimum((c // 128) * 128, IMG - 256), 128)
        window = held[pl.ds(r0, 80), pl.ds(c0, 256)].astype(F32)
        turned = pltpu.roll(window, 256 - (c - c0), 1)[:, :128]
        strip[p % 8] = turned
        upper = strip[p % 8, pl.ds(r - r0, 32), :]
        lower = strip[p % 8, pl.ds(r - r0 + 32, 32), :]
        packed = jnp.where(left_half, upper, pltpu.roll(lower, 64, 1))
        out[p] = jnp.concatenate([packed, parts], 0).astype(BF16)
        return carry

    lax.fori_loop(0, NP, one, 0, unroll=8)


def cut(images, anchors, angle, focus, warp):
    smem = pl.BlockSpec(memory_space=pltpu.SMEM)
    return pl.pallas_call(
        cut_kernel,
        out_shape=jax.ShapeDtypeStruct((NP, 40, 128), BF16),
        in_specs=[smem, smem, smem, smem, pl.BlockSpec(memory_space=pl.ANY)],
        out_specs=pl.BlockSpec(memory_space=pltpu.VMEM),
        scratch_shapes=[
            pltpu.VMEM((IMG, IMG), BF16),
            pltpu.SemaphoreType.DMA,
            pltpu.VMEM((8, 80, 128), F32),
        ],
        compiler_params=pltpu.CompilerParams(vmem_limit_bytes=55 << 20),
    )(jnp.transpose(anchors, (0, 1, 3, 2)), angle, focus, warp, images)


def work_kernel(
    slot,
    euler,
    incoming,
    centers,
    amplitudes,
    widths,
    right_hi,
    right_lo,
    left,
    joiner,
    chooser,
    aux,
    keep,
    send,
    xs,
    base,
    step,
    nyq,
    nyqk,
    env,
    acc,
    model,
    spectra,
    mats,
    zsc,
    focus,
    cols,
    out,
    received,
    sem,
):
    copy = pltpu.make_async_copy(incoming, received, sem)
    copy.start()
    copy.wait()
    prm = jnp.sum(received[:, 32:40, :].astype(F32), axis=1)
    focus[...] = jnp.broadcast_to(prm[:, 1:2], (NT, 128))
    ct, st = cos_sin_turns(prm * (0.5 / math.pi))
    firsts = (ct[:, 0:1], st[:, 0:1])
    rest = (1.0 + prm[:, 2:3], prm[:, 3:4], prm[:, 4:5], 1.0 + prm[:, 5:6])
    shifts = (20.0 * prm[:, 6:7], 20.0 * prm[:, 7:8])
    for i, column in enumerate(firsts + rest + shifts):
        cols[i] = jnp.broadcast_to(column, (NT, 128))
    mine = slot[0]
    turn = []
    for i in range(3):
        angle = jnp.full((8, 128), euler[i, 0, mine], F32)
        c, s = cos_sin_turns(angle * (0.5 / math.pi))
        turn.append((c[0:1, 0:1], s[0:1, 0:1]))
    (ca, sa), (cb, sb), (cc, sc) = turn

    def rotated(sl):
        x, y, z = centers[0:1, sl], centers[1:2, sl], centers[2:3, sl]
        x, y = cc * x - sc * y, sc * x + cc * y
        x, z = cb * x + sb * z, cb * z - sb * x
        x, y = ca * x - sa * y, sa * x + ca * y
        return x, y, z

    blur = 2.0 * math.pi**2 / BOX**2
    freq8 = lax.broadcasted_iota(jnp.int32, (8, CH), 0).astype(F32)
    freq32 = lax.broadcasted_iota(jnp.int32, (32, CH), 0).astype(F32)
    first = lax.broadcasted_iota(jnp.int32, (8, CH), 0) == 0

    def prepare(c, carry):
        sl = pl.ds(pl.multiple_of(c * CH, CH), CH)
        r0, r1, r2 = rotated(sl)
        ct, st, a00, a01, a10, a11, sh_x, sh_y = (
            jnp.concatenate([cols[i]] * (CH // 128), 1) for i in range(8)
        )
        px = ct * r0 + st * r2
        ux = (a00 * px + a01 * r1 + sh_x) * (1.0 / BOX) + 0.5
        uy = (a10 * px + a11 * r1 + sh_y) * (1.0 / BOX) + 0.5
        wide = -blur * widths[0:1, sl] * widths[0:1, sl]
        damp = jnp.exp(wide * (freq32 * freq32))
        env[0, :, sl] = damp
        env[1, :, sl] = amplitudes[0:1, sl] * damp
        damp32 = jnp.exp(wide * 1024.0)
        for axis, u in ((0, ux), (1, uy)):
            u = u - jnp.round(u)
            c1, s1 = cos_sin_turns(u)
            def twice(p):
                return 1.0 - 2.0 * (p[1] * p[1]), 2.0 * (p[0] * p[1])

            def times(p, q):
                return p[0] * q[0] - p[1] * q[1], p[0] * q[1] + p[1] * q[0]

            e1 = (c1, s1)
            e2 = twice(e1)
            e3 = times(e2, e1)
            e4 = twice(e2)
            e5 = times(e4, e1)
            e6 = twice(e3)
            e7 = times(e4, e3)
            c8, s8 = e8 = twice(e4)
            cn, sn = twice(twice(e8))
            d32 = damp32 if axis == 0 else amplitudes[0:1, sl] * damp32
            nyq[2 * axis, :, sl] = cn * d32
            nyq[2 * axis + 1, :, sl] = sn * d32
            step[2 * axis, :, sl] = c8
            step[2 * axis + 1, :, sl] = s8
            e0 = (jnp.ones_like(c1), jnp.zeros_like(c1))
            for j, e in enumerate((e0, e1, e2, e3, e4, e5, e6, e7)):
                for i in range(CH // 128):
                    tile = c * (CH // 128) + i
                    lanes = slice(i * 128, i * 128 + 128)
                    base[2 * axis, tile, pl.ds(j, NT, stride=8), :] = e[0][:, lanes]
                    base[2 * axis + 1, tile, pl.ds(j, NT, stride=8), :] = e[1][:, lanes]
        return carry

    lax.fori_loop(0, NCH, prepare, 0)

    blank = jnp.zeros((24, CH), F32)

    def factors(k, axis, c):
        sl = slice(c * CH, (c + 1) * CH)
        k8 = pl.multiple_of(k * 8, 8)
        tiles = range(c * (CH // 128), (c + 1) * (CH // 128))
        gc = jnp.concatenate([base[2 * axis, t, pl.ds(k8, 8), :] for t in tiles], 1)
        gs = jnp.concatenate([base[2 * axis + 1, t, pl.ds(k8, 8), :] for t in tiles], 1)
        rc = step[2 * axis, pl.ds(k, 1), sl]
        rs = step[2 * axis + 1, pl.ds(k, 1), sl]
        cs, ss = [], []
        for m in range(4):
            damp = env[axis, 8 * m : 8 * m + 8, sl]
            cm, sm = damp * gc, damp * gs
            xs[k, axis * 64 + 8 * m : axis * 64 + 8 * m + 8, sl] = cm
            xs[k, axis * 64 + 32 + 8 * m : axis * 64 + 40 + 8 * m, sl] = sm
            cs.append(cm)
            ss.append(sm)
            if m < 3:
                gc, gs = gc * rc - gs * rs, gc * rs + gs * rc
        return cs, ss

    def ends_of(k, axis, sl):
        cn = jnp.where(first, nyq[2 * axis, pl.ds(k, 1), sl], 0.0)
        sn = jnp.where(first, nyq[2 * axis + 1, pl.ds(k, 1), sl], 0.0)
        return [cn], [sn]

    def forward(b, carry):
        total = jnp.zeros((2 * ROWS, 256), F32)
        for c in range(NCH):
            sl = slice(c * CH, (c + 1) * CH)
            left_rows, right_rows = [], []
            for k in (2 * b, 2 * b + 1):
                cs, ss = factors(k, 0, c)
                cn, sn = ends_of(k, 0, sl)
                left_rows += cs + cn + ss + sn
                cs, ss = factors(k, 1, c)
                cn, sn = ends_of(k, 1, sl)
                right_rows += cs + cn + [blank] + ss + sn + [blank]
            total = total + lax.dot_general(
                jnp.concatenate(left_rows, 0).astype(BF16),
                jnp.concatenate(right_rows, 0).astype(BF16),
                (((1,), (1,)), ((), ())),
                preferred_element_type=F32,
            )
        model[2 * b] = total[:ROWS, :128]
        model[2 * b + 1] = total[ROWS:, 128:]
        return carry

    lax.fori_loop(0, NT // 2, forward, 0, unroll=UF)

    for b in range(4):
        rows = received[8 * b : 8 * b + 8, 0:32, :].reshape(256, 128)
        zsc[256 * b : 256 * b + 256, :] = jnp.dot(
            rows, right_hi[...], preferred_element_type=F32
        ) + jnp.dot(rows, right_lo[...], preferred_element_type=F32)

    lane = lax.broadcasted_iota(jnp.int32, (HALF, 128), 1)
    sign = jnp.where(lane < 64, 1.0, -1.0)

    def swap(x):
        return pltpu.roll(x, 64, 1)

    def spectrum(k, sums):
        z = zsc[pl.ds(pl.multiple_of(k * 32, 32), 32), :]
        z = jnp.concatenate([z[:, :128], z[:, 128:]], 0)
        z_hi, z_lo = split(z)
        p = jnp.dot(left[...], jnp.concatenate([z_hi, z_lo, z_hi], 0), preferred_element_type=F32)
        pc, ps = p[:HALF], swap(p[HALF:])
        spectra[k, :HALF] = pc
        spectra[k, HALF:] = ps
        plus, minus = sign * pc - ps, pc + sign * ps
        return sums[0] + plus * plus, sums[1] + minus * minus

    nought = jnp.zeros((HALF, 128), F32)
    plus, minus = lax.fori_loop(0, NT, spectrum, (nought, nought), unroll=US)
    f_plus = aux[1] / (0.25 + (plus + swap(plus)) * (1.0 / NT))
    f_minus = aux[2] / (0.25 + (minus + swap(minus)) * (1.0 / NT))
    radius = aux[0]

    def residual(k, carry):
        x = focus[pl.ds(k, 1), :] * radius * (1.0 / BOX) + 0.1
        n = jnp.round(x * (0.5 / math.pi))
        r = (x - n * 6.28125) - n * (2.0 * math.pi - 6.28125)
        ctf = -cos_sin_turns(r * (0.5 / math.pi))[1]
        dc = spectra[k, :HALF] - ctf * model[k, :HALF]
        ds = spectra[k, HALF:] - ctf * swap(model[k, HALF:])
        hp = (f_plus * ctf) * (sign * dc - ds)
        hm = (f_minus * ctf) * (dc + sign * ds)
        m1 = jnp.concatenate([hm, swap(sign * hm)], 0).astype(BF16)
        m2 = jnp.concatenate([sign * hp, -swap(hp)], 0).astype(BF16)
        mats[k, 0] = jnp.dot(
            jnp.concatenate([m1, m2], 1), joiner[...], preferred_element_type=F32
        ).astype(BF16)
        mats[k, 1] = lax.dot_general(
            chooser[...],
            jnp.concatenate([m1, m2], 0),
            (((1,), (1,)), ((), ())),
            preferred_element_type=F32,
        ).astype(BF16)
        return carry

    lax.fori_loop(0, NT, residual, 0, unroll=UR)

    acc[...] = jnp.zeros_like(acc)
    w1 = [freq8 + float(8 * m) for m in range(4)]
    w2 = [w * w for w in w1]

    def backward(k, carry):
        k8 = pl.multiple_of(k * 8, 8)
        for c in range(NCH):
            sl = slice(c * CH, (c + 1) * CH)
            sides, parts = [], []
            for axis in (0, 1):
                cs = [xs[k, axis * 64 + 8 * m : axis * 64 + 8 * m + 8, sl] for m in range(4)]
                ss = [xs[k, axis * 64 + 32 + 8 * m : axis * 64 + 40 + 8 * m, sl] for m in range(4)]
                cn, sn = ends_of(k, axis, sl)
                parts.append((cs, ss))
                sides.append(jnp.concatenate(cs + cn + ss + sn, 0).astype(BF16))
            backs = [
                jnp.dot(
                    mats[k, axis],
                    jnp.concatenate([sides[1 - axis]] * 2, 0),
                    preferred_element_type=F32,
                )
                for axis in (0, 1)
            ]
            width_sum = acc[0, :, sl]
            value_sum = acc[1, :, sl]
            moves = [None, None]
            for m in range(4):
                values = []
                for axis in (0, 1):
                    c_m, s_m = parts[axis][0][m], parts[axis][1][m]
                    kc = backs[axis][8 * m : 8 * m + 8]
                    ks = backs[axis][HALF + 8 * m : HALF + 8 * m + 8]
                    values.append(c_m * kc + s_m * ks)
                    move = w1[m] * (c_m * ks - s_m * kc)
                    moves[axis] = move if m == 0 else moves[axis] + move
                value_sum = value_sum + values[1]
                width_sum = width_sum + w2[m] * (values[0] + values[1])
            acc[0, :, sl] = width_sum
            acc[1, :, sl] = value_sum
            for axis in (0, 1):
                for i in range(CH // 128):
                    lanes = slice(i * 128, i * 128 + 128)
                    base[axis, c * (CH // 128) + i, pl.ds(k8, 8), :] = moves[axis][:, lanes]
                nyqk[2 * axis, pl.ds(k, 1), sl] = backs[axis][32:33]
                nyqk[2 * axis + 1, pl.ds(k, 1), sl] = backs[axis][HALF + 32 : HALF + 33]
        return carry

    lax.fori_loop(0, NT, backward, 0, unroll=UB)

    terms = [jnp.zeros((NT, 128), F32) for _ in range(6)]
    unit = 2.0 * math.pi / BOX
    ct, st, a00, a01, a10, a11 = (cols[i] for i in range(6))
    for c in range(G // 128):
        sl = slice(c * 128, (c + 1) * 128)
        moves, ends = [], []
        for axis in (0, 1):
            move = base[axis, c, pl.ds(0, NT, stride=8), :]
            for j in range(1, 8):
                move = move + base[axis, c, pl.ds(j, NT, stride=8), :]
            nc, ns = nyq[2 * axis, :, sl], nyq[2 * axis + 1, :, sl]
            kc, ks = nyqk[2 * axis, :, sl], nyqk[2 * axis + 1, :, sl]
            moves.append(unit * (move + 32.0 * (nc * ks - ns * kc)))
            ends.append(jnp.sum(nc * kc + ns * ks, axis=0, keepdims=True))
        mx, my = moves
        r0, r1, r2 = rotated(sl)
        px = ct * r0 + st * r2
        for i, t in enumerate((mx * px, mx * r1, my * px, my * r1, mx, my)):
            terms[i] = terms[i] + t
        vx = a00 * mx + a10 * my
        vy = a01 * mx + a11 * my
        x = jnp.sum(ct * vx, axis=0, keepdims=True)
        z = jnp.sum(st * vx, axis=0, keepdims=True)
        y = jnp.sum(vy, axis=0, keepdims=True)
        x, y = ca * x + sa * y, ca * y - sa * x
        x, z = cb * x - sb * z, sb * x + cb * z
        x, y = cc * x + sc * y, cc * y - sc * x
        curve = jnp.sum(acc[0, :, sl], axis=0, keepdims=True) + 1024.0 * (ends[0] + ends[1])
        value = jnp.sum(acc[1, :, sl], axis=0, keepdims=True) + ends[1]
        half, lanes = c // 8, slice((c % 8) * 128, (c % 8) * 128 + 128)
        out[half, 0:1, lanes] = x
        out[half, 1:2, lanes] = y
        out[half, 2:3, lanes] = z
        out[half, 3:4, lanes] = value / amplitudes[0:1, sl]
        out[half, 4:5, lanes] = (-2.0 * blur) * widths[0:1, sl] * curve
    lane_w = lax.broadcasted_iota(jnp.int32, (NT, 128), 1)
    warp_rows = jnp.zeros((NT, 128), F32)
    for i in range(6):
        total = jnp.sum(terms[i], axis=1, keepdims=True) * (20.0 if i > 3 else 1.0)
        warp_rows = jnp.where(lane_w == i, total, warp_rows)
    for k in range(NT):
        i = k // 2
        out[k % 2, 5 + i // 8 : 6 + i // 8, (i % 8) * 128 : (i % 8) * 128 + 128] = warp_rows[k : k + 1]
    core = mine % 2
    keep[...] = out[core]
    send[...] = out[1 - core]


def work(slot, euler, received, centers, amplitudes, widths):
    smem = pl.BlockSpec(memory_space=pltpu.SMEM)
    vmem = pl.BlockSpec(memory_space=pltpu.VMEM)
    right_hi, right_lo, left, joiner, chooser, aux = tables()
    return pl.pallas_call(
        work_kernel,
        out_shape=[jax.ShapeDtypeStruct((8, G // 2), F32)] * 2,
        in_specs=[smem, smem, pl.BlockSpec(memory_space=pl.ANY)] + [vmem] * 9,
        out_specs=[vmem, vmem],
        scratch_shapes=[
            pltpu.VMEM((NT, 128, G), F32),
            pltpu.VMEM((4, G // 128, NT * 8, 128), F32),
            pltpu.VMEM((4, NT, G), F32),
            pltpu.VMEM((4, NT, G), F32),
            pltpu.VMEM((4, NT, G), F32),
            pltpu.VMEM((2, 32, G), F32),
            pltpu.VMEM((2, 8, G), F32),
            pltpu.VMEM((NT, ROWS, 128), F32),
            pltpu.VMEM((NT, ROWS, 128), F32),
            pltpu.VMEM((NT, 2, ROWS, 2 * ROWS), BF16),
            pltpu.VMEM((1024, 256), F32),
            pltpu.VMEM((NT, 128), F32),
            pltpu.VMEM((8, NT, 128), F32),
            pltpu.VMEM((2, 8, G // 2), F32),
            pltpu.VMEM((NT, 40, 128), BF16),
            pltpu.SemaphoreType.DMA,
        ],
        compiler_params=pltpu.CompilerParams(vmem_limit_bytes=55 << 20),
    )(
        slot,
        jnp.transpose(euler, (1, 0, 2)),
        received,
        centers,
        amplitudes.reshape(1, G),
        widths.reshape(1, G),
        jnp.asarray(right_hi),
        jnp.asarray(right_lo),
        jnp.asarray(left),
        jnp.asarray(joiner),
        jnp.asarray(chooser),
        jnp.asarray(aux),
    )


def exchanged(value, axis, masks):
    size = lax.axis_size(axis)
    return lax.ppermute(value, axis, [(i, i ^ masks[i % 2]) for i in range(size)])


def on_device(tilt_images, anchors, euler, tilt_angle, defocus, warp, centers, amplitudes, widths):
    payload = cut(tilt_images, anchors, tilt_angle, defocus, warp)
    received = lax.all_to_all(payload, "tilt", split_axis=0, concat_axis=0, tiled=True)
    index = lax.axis_index("tilt").astype(jnp.int32)
    total, other = work(index.reshape(1), euler, received, centers, amplitudes, widths)
    total = total + exchanged(other, "tilt", (1, 1))
    for masks in ((2, 8), (6, 24), (8, 2), (24, 6)):
        total = total + exchanged(total, "tilt", masks)
    place = index // 2
    warp_local = lax.dynamic_slice(total, (5 + place // 8, (place % 8) * 128), (1, 6))
    for mask in (1, 2, 6):
        total = total + exchanged(total, "tomo", (mask, mask))
    other = exchanged(total, "tilt", (1, 1))
    first = index % 2 == 0
    template = jnp.concatenate(
        [jnp.where(first, total, other)[:5], jnp.where(first, other, total)[:5]], 1
    )
    return (template, warp_local.reshape(1, 1, 6))


def solution(mesh):
    placed = (
        P("tomo", "tilt", None, None),
        P("tomo", "tilt", None, None),
        P("tomo", None, None),
        P("tomo", "tilt"),
        P("tomo", "tilt"),
        P("tomo", "tilt", None),
        P(),
        P(),
        P(),
    )
    return jax.shard_map(
        on_device,
        mesh=mesh,
        in_specs=placed,
        out_specs=(P(), P("tomo", "tilt", None)),
        check_vma=False,
    )
```

```python
import math

import jax
import jax.numpy as jnp
import numpy as np
from jax import lax
from jax.experimental import pallas as pl
from jax.experimental.pallas import tpu as pltpu
from jax.sharding import PartitionSpec as P

G = 2048
BOX = 64
IMG = 1024
NT = 32
NP = 32
SHARES = 16
CHUNK = G // SHARES
CH = 256
NCH = G // CH
HALF = 40
ROWS = 2 * HALF
UF, UB = 3, 4
F32 = jnp.float32
BF16 = jnp.bfloat16


def _fit(fn, degree):
    n = 64
    nodes = 0.125 * (1 + np.cos(np.pi * (np.arange(n) + 0.5) / n))
    return [float(c) for c in np.polynomial.polynomial.polyfit(nodes, fn(np.sqrt(nodes)), degree)]


SIN_POLY = _fit(lambda u: np.sin(np.pi * u) / u, 5)
COS_POLY = _fit(lambda u: np.cos(np.pi * u), 5)


def _horner(w, coefs):
    acc = jnp.full_like(w, coefs[-1])
    for c in coefs[-2::-1]:
        acc = acc * w + c
    return acc


def cos_sin_turns(turns):
    u = turns - jnp.round(turns)
    w = u * u
    s = u * _horner(w, SIN_POLY)
    c = _horner(w, COS_POLY)
    return 1.0 - 2.0 * (s * s), 2.0 * (s * c)


def split(x):
    hi = x.astype(BF16)
    return hi, (x - hi.astype(F32)).astype(BF16)


def np_split(x):
    hi = x.astype(jnp.bfloat16)
    lo = (x - hi.astype(np.float64)).astype(jnp.bfloat16)
    return hi, lo


def tables():
    pos = np.arange(BOX)
    freq = np.arange(33)
    ang = 2 * np.pi * ((pos[:, None] * freq[None, :]) % BOX) / BOX
    lanes = np.zeros((BOX, 128))
    lanes[:, :33] = np.cos(ang)
    lanes[:, 64:97] = np.sin(ang)
    right = np.zeros((128, 256))
    right[:64, :128] = lanes
    right[64:, 128:] = lanes
    right_hi, right_lo = np_split(right)
    rows = np.zeros((ROWS, BOX))
    rows[:33] = np.cos(ang).T / BOX
    rows[HALF : HALF + 33] = np.sin(ang).T / BOX
    left_hi, left_lo = np_split(rows)
    left = np.concatenate([left_hi, left_hi, left_lo], 1)
    phi = np.ones(33)
    phi[0] = phi[32] = 0.5
    both = -4.0 / (NT * NP) * phi[:, None] * phi[None, :]
    plus, minus = both.copy(), both.copy()
    plus[32, 32] *= 2.0
    minus[32, 32] = 0.0
    aux = np.zeros((3, HALF, 128), np.float32)
    for base in (0, 64):
        aux[0, :33, base : base + 33] = freq[:, None] ** 2 + freq[None, :] ** 2
        aux[1, :33, base : base + 33] = plus
        aux[2, :33, base : base + 33] = minus
    joiner = np.zeros((256, 2 * ROWS), jnp.bfloat16)
    chooser = np.zeros((ROWS, 128), jnp.bfloat16)
    for i in range(HALF):
        for part in (0, 1):
            joiner[128 * part + i, ROWS * part + i] = 1
            joiner[128 * part + 64 + i, ROWS * part + HALF + i] = 1
        chooser[i, i] = 1
        chooser[HALF + i, 64 + i] = 1
    return right_hi, right_lo, left, joiner, chooser, aux


def cut_kernel(anchor, angle, focus, warp, image, out, held, sem, strip):
    bands = [pl.ds(i * (IMG // 8), IMG // 8) for i in range(8)]
    copies = [
        pltpu.make_async_copy(image.at[0, 0, band], held.at[band], sem.at[i])
        for i, band in enumerate(bands)
    ]
    for copy in copies:
        copy.start()
    lane = lax.broadcasted_iota(jnp.int32, (8, 128), 1)
    sub = lax.broadcasted_iota(jnp.int32, (8, 128), 0)
    values = [angle[0, 0], focus[0, 0]] + [warp[0, 0, i] for i in range(6)]
    row = jnp.zeros((8, 128), F32)
    for i, v in enumerate(values):
        row = jnp.where(lane == i, v, row)
    hi = row.astype(BF16).astype(F32)
    mid = (row - hi).astype(BF16).astype(F32)
    low = row - hi - mid
    parts = jnp.where(sub == 0, hi, jnp.where(sub == 1, mid, jnp.where(sub == 2, low, 0.0)))
    left_half = lax.broadcasted_iota(jnp.int32, (32, 128), 1) < BOX

    for copy in copies:
        copy.wait()

    def one(p, carry):
        r, c = anchor[0, 0, 0, p], anchor[0, 0, 1, p]
        r0 = pl.multiple_of(jnp.minimum((r // 16) * 16, IMG - 80), 16)
        c0 = pl.multiple_of(jnp.minimum((c // 128) * 128, IMG - 256), 128)
        window = held[pl.ds(r0, 80), pl.ds(c0, 256)].astype(F32)
        turned = pltpu.roll(window, 256 - (c - c0), 1)[:, :128]
        strip[p % 8] = turned
        upper = strip[p % 8, pl.ds(r - r0, 32), :]
        lower = strip[p % 8, pl.ds(r - r0 + 32, 32), :]
        packed = jnp.where(left_half, upper, pltpu.roll(lower, 64, 1))
        out[p] = jnp.concatenate([packed, parts], 0).astype(BF16)
        return carry

    lax.fori_loop(0, NP, one, 0, unroll=8)


def cut(images, anchors, angle, focus, warp):
    smem = pl.BlockSpec(memory_space=pltpu.SMEM)
    return pl.pallas_call(
        cut_kernel,
        out_shape=jax.ShapeDtypeStruct((NP, 40, 128), BF16),
        in_specs=[smem, smem, smem, smem, pl.BlockSpec(memory_space=pl.ANY)],
        out_specs=pl.BlockSpec(memory_space=pltpu.VMEM),
        scratch_shapes=[
            pltpu.VMEM((IMG, IMG), BF16),
            pltpu.SemaphoreType.DMA((8,)),
            pltpu.VMEM((8, 80, 128), F32),
        ],
        compiler_params=pltpu.CompilerParams(vmem_limit_bytes=55 << 20),
    )(jnp.transpose(anchors, (0, 1, 3, 2)), angle, focus, warp, images)


def work_kernel(
    slot,
    euler,
    incoming,
    centers,
    amplitudes,
    widths,
    right_hi,
    right_lo,
    left,
    joiner,
    chooser,
    aux,
    out,
    xs,
    base,
    step,
    nyq,
    nyqk,
    env,
    acc,
    model,
    spectra,
    mats,
    focus,
    cols,
    received,
    raw,
    sem,
):
    copy = pltpu.make_async_copy(incoming, received, sem)
    copy.start()
    copy.wait()
    raw[...] = received[:, 32:40, :].astype(F32).reshape(NT * 8, 128)
    prm = raw[pl.ds(0, NT, stride=8), :] + raw[pl.ds(1, NT, stride=8), :]
    prm = prm + raw[pl.ds(2, NT, stride=8), :]
    focus[...] = jnp.broadcast_to(prm[:, 1:2], (NT, 128))
    ct, st = cos_sin_turns(prm * (0.5 / math.pi))
    firsts = (ct[:, 0:1], st[:, 0:1])
    rest = (1.0 + prm[:, 2:3], prm[:, 3:4], prm[:, 4:5], 1.0 + prm[:, 5:6])
    shifts = (20.0 * prm[:, 6:7], 20.0 * prm[:, 7:8])
    for i, column in enumerate(firsts + rest + shifts):
        cols[i] = jnp.broadcast_to(column, (NT, 128))
    mine = slot[0]
    turn = []
    for i in range(3):
        angle = jnp.full((8, 128), euler[i, 0, mine], F32)
        c, s = cos_sin_turns(angle * (0.5 / math.pi))
        turn.append((c[0:1, 0:1], s[0:1, 0:1]))
    (ca, sa), (cb, sb), (cc, sc) = turn

    def rotated(sl):
        x, y, z = centers[0:1, sl], centers[1:2, sl], centers[2:3, sl]
        x, y = cc * x - sc * y, sc * x + cc * y
        x, z = cb * x + sb * z, cb * z - sb * x
        x, y = ca * x - sa * y, sa * x + ca * y
        return x, y, z

    blur = 2.0 * math.pi**2 / BOX**2
    freq8 = lax.broadcasted_iota(jnp.int32, (8, CH), 0).astype(F32)
    freq32 = lax.broadcasted_iota(jnp.int32, (32, CH), 0).astype(F32)
    first = lax.broadcasted_iota(jnp.int32, (8, CH), 0) == 0

    lane = lax.broadcasted_iota(jnp.int32, (HALF, 128), 1)
    sign = jnp.where(lane < 64, 1.0, -1.0)

    def swap(x):
        return pltpu.roll(x, 64, 1)

    def spectrum(c, sums):
        rows = received[pl.ds(c * 4, 4), 0:32, :].reshape(128, 128)
        halves = jnp.dot(rows, right_hi[...], preferred_element_type=F32)
        halves = halves + jnp.dot(rows, right_lo[...], preferred_element_type=F32)
        for i in range(4):
            z = halves[32 * i : 32 * i + 32]
            z = jnp.concatenate([z[:, :128], z[:, 128:]], 0)
            z_hi, z_lo = split(z)
            p = jnp.dot(
                left[...], jnp.concatenate([z_hi, z_lo, z_hi], 0), preferred_element_type=F32
            )
            pc, ps = p[:HALF], swap(p[HALF:])
            spectra[c * 4 + i, :HALF] = pc
            spectra[c * 4 + i, HALF:] = ps
            plus, minus = sign * pc - ps, pc + sign * ps
            sums = sums[0] + plus * plus, sums[1] + minus * minus
        return sums

    def prepare(c, sums):
        sl = pl.ds(pl.multiple_of(c * CH, CH), CH)
        r0, r1, r2 = rotated(sl)
        ct, st, a00, a01, a10, a11, sh_x, sh_y = (
            jnp.concatenate([cols[i]] * (CH // 128), 1) for i in range(8)
        )
        px = ct * r0 + st * r2
        ux = (a00 * px + a01 * r1 + sh_x) * (1.0 / BOX) + 0.5
        uy = (a10 * px + a11 * r1 + sh_y) * (1.0 / BOX) + 0.5
        wide = -blur * widths[0:1, sl] * widths[0:1, sl]
        damp = jnp.exp(wide * (freq32 * freq32))
        env[0, :, sl] = damp
        env[1, :, sl] = amplitudes[0:1, sl] * damp
        damp32 = jnp.exp(wide * 1024.0)
        for axis, u in ((0, ux), (1, uy)):
            u = u - jnp.round(u)
            c1, s1 = cos_sin_turns(u)
            def twice(p):
                return 1.0 - 2.0 * (p[1] * p[1]), 2.0 * (p[0] * p[1])

            def times(p, q):
                return p[0] * q[0] - p[1] * q[1], p[0] * q[1] + p[1] * q[0]

            e1 = (c1, s1)
            e2 = twice(e1)
            e3 = times(e2, e1)
            e4 = twice(e2)
            e5 = times(e4, e1)
            e6 = twice(e3)
            e7 = times(e4, e3)
            c8, s8 = e8 = twice(e4)
            cn, sn = twice(twice(e8))
            d32 = damp32 if axis == 0 else amplitudes[0:1, sl] * damp32
            nyq[2 * axis, :, sl] = cn * d32
            nyq[2 * axis + 1, :, sl] = sn * d32
            step[2 * axis, :, sl] = c8
            step[2 * axis + 1, :, sl] = s8
            e0 = (jnp.ones_like(c1), jnp.zeros_like(c1))
            for j, e in enumerate((e0, e1, e2, e3, e4, e5, e6, e7)):
                for i in range(CH // 128):
                    tile = c * (CH // 128) + i
                    lanes = slice(i * 128, i * 128 + 128)
                    base[2 * axis, tile, pl.ds(j, NT, stride=8), :] = e[0][:, lanes]
                    base[2 * axis + 1, tile, pl.ds(j, NT, stride=8), :] = e[1][:, lanes]
        return spectrum(c, sums)

    nought = jnp.zeros((HALF, 128), F32)
    plus, minus = lax.fori_loop(0, NCH, prepare, (nought, nought), unroll=2)
    f_plus = aux[1] / (0.25 + (plus + swap(plus)) * (1.0 / NT))
    f_minus = aux[2] / (0.25 + (minus + swap(minus)) * (1.0 / NT))
    radius = aux[0]

    blank = jnp.zeros((24, CH), F32)

    def factors(k, axis, c):
        sl = slice(c * CH, (c + 1) * CH)
        k8 = pl.multiple_of(k * 8, 8)
        tiles = range(c * (CH // 128), (c + 1) * (CH // 128))
        gc = jnp.concatenate([base[2 * axis, t, pl.ds(k8, 8), :] for t in tiles], 1)
        gs = jnp.concatenate([base[2 * axis + 1, t, pl.ds(k8, 8), :] for t in tiles], 1)
        rc = step[2 * axis, pl.ds(k, 1), sl]
        rs = step[2 * axis + 1, pl.ds(k, 1), sl]
        cs, ss = [], []
        for m in range(4):
            damp = env[axis, 8 * m : 8 * m + 8, sl]
            cm, sm = damp * gc, damp * gs
            xs[k, axis * 64 + 8 * m : axis * 64 + 8 * m + 8, sl] = cm
            xs[k, axis * 64 + 32 + 8 * m : axis * 64 + 40 + 8 * m, sl] = sm
            cs.append(cm)
            ss.append(sm)
            if m < 3:
                gc, gs = gc * rc - gs * rs, gc * rs + gs * rc
        return cs, ss

    def ends_of(k, axis, sl):
        cn = jnp.where(first, nyq[2 * axis, pl.ds(k, 1), sl], 0.0)
        sn = jnp.where(first, nyq[2 * axis + 1, pl.ds(k, 1), sl], 0.0)
        return [cn], [sn]

    def forward(b):
        total = jnp.zeros((2 * ROWS, 256), F32)
        for c in range(NCH):
            sl = slice(c * CH, (c + 1) * CH)
            left_rows, right_rows = [], []
            for k in (2 * b, 2 * b + 1):
                cs, ss = factors(k, 0, c)
                cn, sn = ends_of(k, 0, sl)
                left_rows += cs + cn + ss + sn
                cs, ss = factors(k, 1, c)
                cn, sn = ends_of(k, 1, sl)
                right_rows += cs + cn + [blank] + ss + sn + [blank]
            total = total + lax.dot_general(
                jnp.concatenate(left_rows, 0).astype(BF16),
                jnp.concatenate(right_rows, 0).astype(BF16),
                (((1,), (1,)), ((), ())),
                preferred_element_type=F32,
            )
        model[2 * b] = total[:ROWS, :128]
        model[2 * b + 1] = total[ROWS:, 128:]

    def residual(k):
        x = focus[pl.ds(k, 1), :] * radius * (1.0 / BOX) + 0.1
        n = jnp.round(x * (0.5 / math.pi))
        r = (x - n * 6.28125) - n * (2.0 * math.pi - 6.28125)
        ctf = -cos_sin_turns(r * (0.5 / math.pi))[1]
        dc = spectra[k, :HALF] - ctf * model[k, :HALF]
        ds = spectra[k, HALF:] - ctf * swap(model[k, HALF:])
        hp = (f_plus * ctf) * (sign * dc - ds)
        hm = (f_minus * ctf) * (dc + sign * ds)
        m1 = jnp.concatenate([hm, swap(sign * hm)], 0).astype(BF16)
        m2 = jnp.concatenate([sign * hp, -swap(hp)], 0).astype(BF16)
        mats[k, 0] = jnp.dot(
            jnp.concatenate([m1, m2], 1), joiner[...], preferred_element_type=F32
        ).astype(BF16)
        mats[k, 1] = lax.dot_general(
            chooser[...],
            jnp.concatenate([m1, m2], 0),
            (((1,), (1,)), ((), ())),
            preferred_element_type=F32,
        ).astype(BF16)

    def pair(b, carry):
        forward(b + 1)
        residual(2 * b)
        residual(2 * b + 1)
        return carry

    forward(0)
    lax.fori_loop(0, NT // 2 - 1, pair, 0, unroll=UF)
    residual(NT - 2)
    residual(NT - 1)

    acc[...] = jnp.zeros_like(acc)
    w1 = [freq8 + float(8 * m) for m in range(4)]
    w2 = [w * w for w in w1]

    def backward(k, carry):
        k8 = pl.multiple_of(k * 8, 8)
        for c in range(NCH):
            sl = slice(c * CH, (c + 1) * CH)
            sides, parts = [], []
            for axis in (0, 1):
                cs = [xs[k, axis * 64 + 8 * m : axis * 64 + 8 * m + 8, sl] for m in range(4)]
                ss = [xs[k, axis * 64 + 32 + 8 * m : axis * 64 + 40 + 8 * m, sl] for m in range(4)]
                cn, sn = ends_of(k, axis, sl)
                parts.append((cs, ss))
                sides.append(jnp.concatenate(cs + cn + ss + sn, 0).astype(BF16))
            width_sum = acc[0, :, sl]
            for axis in (0, 1):
                back = jnp.dot(
                    mats[k, axis],
                    jnp.concatenate([sides[1 - axis]] * 2, 0),
                    preferred_element_type=F32,
                )
                cs, ss = parts[axis]
                move = None
                value_sum = acc[1, :, sl] if axis == 1 else None
                for m in range(4):
                    kc = back[8 * m : 8 * m + 8]
                    ks = back[HALF + 8 * m : HALF + 8 * m + 8]
                    re = cs[m] * kc + ss[m] * ks
                    im = w1[m] * (cs[m] * ks - ss[m] * kc)
                    width_sum = width_sum + w2[m] * re
                    move = im if m == 0 else move + im
                    if axis == 1:
                        value_sum = value_sum + re
                if axis == 1:
                    acc[1, :, sl] = value_sum
                for t in range(CH // 128):
                    lanes = slice(t * 128, t * 128 + 128)
                    base[axis, c * (CH // 128) + t, pl.ds(k8, 8), :] = move[:, lanes]
                nyqk[2 * axis, pl.ds(k, 1), sl] = back[32:33]
                nyqk[2 * axis + 1, pl.ds(k, 1), sl] = back[HALF + 32 : HALF + 33]
            acc[0, :, sl] = width_sum
        return carry

    lax.fori_loop(0, NT, backward, 0, unroll=UB)

    terms = [jnp.zeros((NT, 128), F32) for _ in range(6)]
    unit = 2.0 * math.pi / BOX
    ct, st, a00, a01, a10, a11 = (cols[i] for i in range(6))
    for c in range(G // 128):
        sl = slice(c * 128, (c + 1) * 128)
        moves, ends = [], []
        for axis in (0, 1):
            move = base[axis, c, pl.ds(0, NT, stride=8), :]
            for j in range(1, 8):
                move = move + base[axis, c, pl.ds(j, NT, stride=8), :]
            nc, ns = nyq[2 * axis, :, sl], nyq[2 * axis + 1, :, sl]
            kc, ks = nyqk[2 * axis, :, sl], nyqk[2 * axis + 1, :, sl]
            moves.append(unit * (move + 32.0 * (nc * ks - ns * kc)))
            ends.append(jnp.sum(nc * kc + ns * ks, axis=0, keepdims=True))
        mx, my = moves
        r0, r1, r2 = rotated(sl)
        px = ct * r0 + st * r2
        for i, t in enumerate((mx * px, mx * r1, my * px, my * r1, mx, my)):
            terms[i] = terms[i] + t
        vx = a00 * mx + a10 * my
        vy = a01 * mx + a11 * my
        x = jnp.sum(ct * vx, axis=0, keepdims=True)
        z = jnp.sum(st * vx, axis=0, keepdims=True)
        y = jnp.sum(vy, axis=0, keepdims=True)
        x, y = ca * x + sa * y, ca * y - sa * x
        x, z = cb * x - sb * z, sb * x + cb * z
        x, y = cc * x + sc * y, cc * y - sc * x
        curve = jnp.sum(acc[0, :, sl], axis=0, keepdims=True) + 1024.0 * (ends[0] + ends[1])
        value = jnp.sum(acc[1, :, sl], axis=0, keepdims=True) + ends[1]
        rows = (x, y, z, value / amplitudes[0:1, sl], (-2.0 * blur) * widths[0:1, sl] * curve)
        for i, row in enumerate(rows):
            out[c, 0:1, i * CHUNK : (i + 1) * CHUNK] = row
    lane_w = lax.broadcasted_iota(jnp.int32, (NT, 128), 1)
    warp_rows = jnp.zeros((NT, 128), F32)
    for i in range(6):
        total = jnp.sum(terms[i], axis=1, keepdims=True) * (20.0 if i > 3 else 1.0)
        warp_rows = jnp.where(lane_w == i, total, warp_rows)
    moved_rows = pltpu.roll(warp_rows, 64, 1)
    for d in range(SHARES):
        k = 2 * d
        out[d, 0:1, 5 * CHUNK : 6 * CHUNK] = warp_rows[k : k + 1] + moved_rows[k + 1 : k + 2]


def work(slot, euler, received, centers, amplitudes, widths):
    smem = pl.BlockSpec(memory_space=pltpu.SMEM)
    vmem = pl.BlockSpec(memory_space=pltpu.VMEM)
    right_hi, right_lo, left, joiner, chooser, aux = tables()
    return pl.pallas_call(
        work_kernel,
        out_shape=jax.ShapeDtypeStruct((SHARES, 1, 6 * CHUNK), F32),
        in_specs=[smem, smem, pl.BlockSpec(memory_space=pl.ANY)] + [vmem] * 9,
        out_specs=vmem,
        scratch_shapes=[
            pltpu.VMEM((NT, 128, G), F32),
            pltpu.VMEM((4, G // 128, NT * 8, 128), F32),
            pltpu.VMEM((4, NT, G), F32),
            pltpu.VMEM((4, NT, G), F32),
            pltpu.VMEM((4, NT, G), F32),
            pltpu.VMEM((2, 32, G), F32),
            pltpu.VMEM((2, 8, G), F32),
            pltpu.VMEM((NT, ROWS, 128), F32),
            pltpu.VMEM((NT, ROWS, 128), F32),
            pltpu.VMEM((NT, 2, ROWS, 2 * ROWS), BF16),
            pltpu.VMEM((NT, 128), F32),
            pltpu.VMEM((8, NT, 128), F32),
            pltpu.VMEM((NT, 40, 128), BF16),
            pltpu.VMEM((NT * 8, 128), F32),
            pltpu.SemaphoreType.DMA,
        ],
        compiler_params=pltpu.CompilerParams(vmem_limit_bytes=55 << 20),
    )(
        slot,
        jnp.transpose(euler, (1, 0, 2)),
        received,
        centers,
        amplitudes.reshape(1, G),
        widths.reshape(1, G),
        jnp.asarray(right_hi),
        jnp.asarray(right_lo),
        jnp.asarray(left),
        jnp.asarray(joiner),
        jnp.asarray(chooser),
        jnp.asarray(aux),
    )


def on_device(tilt_images, anchors, euler, tilt_angle, defocus, warp, centers, amplitudes, widths):
    tomos, cores = lax.axis_size("tomo"), lax.axis_size("tilt") // SHARES
    row = [[(t * SHARES + i) * cores + c for i in range(SHARES)] for t in range(tomos) for c in range(cores)]
    column = [[group[i] for group in row] for i in range(SHARES)]

    def swapped(value, groups):
        return lax.all_to_all(
            value, ("tomo", "tilt"), split_axis=0, concat_axis=0, tiled=True, axis_index_groups=groups
        )

    index = lax.axis_index("tilt").astype(jnp.int32)
    first = lax.axis_index("tomo").astype(jnp.int32) * cores
    at = 5 * CHUNK + (index & 1) * 64
    payload = cut(tilt_images, anchors, tilt_angle, defocus, warp)
    rest = (index, first, at, euler, centers, amplitudes, widths)
    payload, rest = lax.optimization_barrier((payload, rest))
    received = lax.all_to_all(payload, "tilt", split_axis=0, concat_axis=0, tiled=True)
    received, rest = lax.optimization_barrier((received, rest))
    index, first, at, euler, centers, amplitudes, widths = rest
    partial = work(index.reshape(1), euler, received, centers, amplitudes, widths)
    partial, first, at = lax.optimization_barrier((partial, first, at))
    share = jnp.sum(swapped(partial, row), 0, keepdims=True)
    shares = swapped(jnp.broadcast_to(share, (tomos * cores, 1, 6 * CHUNK)), column)
    total = jnp.sum(shares, 0, keepdims=True)
    chunks = swapped(jnp.broadcast_to(total, (SHARES, 1, 6 * CHUNK)), row)
    chunks, shares, first, at = lax.optimization_barrier((chunks, shares, first, at))
    template = chunks[:, 0, : 5 * CHUNK].reshape(SHARES, 5, CHUNK)
    template = jnp.transpose(template, (1, 0, 2)).reshape(5, G)
    warp_local = jnp.sum(lax.dynamic_slice(shares, (first, 0, at), (cores, 1, 6)), 0)
    return (template, warp_local.reshape(1, 1, 6))


def solution(mesh):
    placed = (
        P("tomo", "tilt", None, None),
        P("tomo", "tilt", None, None),
        P("tomo", None, None),
        P("tomo", "tilt"),
        P("tomo", "tilt"),
        P("tomo", "tilt", None),
        P(),
        P(),
        P(),
    )
    return jax.shard_map(
        on_device,
        mesh=mesh,
        in_specs=placed,
        out_specs=(P(), P("tomo", "tilt", None)),
        check_vma=False,
    )
```

```python
import math

import jax
import jax.numpy as jnp
import numpy as np
from jax import lax
from jax.experimental import pallas as pl
from jax.experimental.pallas import tpu as pltpu
from jax.sharding import PartitionSpec as P

G = 2048
BOX = 64
IMG = 1024
NT = 32
NP = 32
SHARES = 16
CHUNK = G // SHARES
CH = 256
NCH = G // CH
HALF = 40
ROWS = 2 * HALF
UF, UB = 3, 8
F32 = jnp.float32
BF16 = jnp.bfloat16


def _fit(fn, degree):
    n = 64
    nodes = 0.125 * (1 + np.cos(np.pi * (np.arange(n) + 0.5) / n))
    return [float(c) for c in np.polynomial.polynomial.polyfit(nodes, fn(np.sqrt(nodes)), degree)]


SIN_POLY = _fit(lambda u: np.sin(np.pi * u) / u, 5)
COS_POLY = _fit(lambda u: np.cos(np.pi * u), 5)


def _horner(w, coefs):
    acc = jnp.full_like(w, coefs[-1])
    for c in coefs[-2::-1]:
        acc = acc * w + c
    return acc


def cos_sin_turns(turns):
    u = turns - jnp.round(turns)
    w = u * u
    s = u * _horner(w, SIN_POLY)
    c = _horner(w, COS_POLY)
    return 1.0 - 2.0 * (s * s), 2.0 * (s * c)


def split(x):
    hi = x.astype(BF16)
    return hi, (x - hi.astype(F32)).astype(BF16)


def np_split(x):
    hi = x.astype(jnp.bfloat16)
    lo = (x - hi.astype(np.float64)).astype(jnp.bfloat16)
    return hi, lo


def tables():
    pos = np.arange(BOX)
    freq = np.append(np.arange(1, 33), 0)
    ang = 2 * np.pi * ((pos[:, None] * freq[None, :]) % BOX) / BOX
    lanes = np.zeros((BOX, 128))
    lanes[:, :33] = np.cos(ang)
    lanes[:, 64:97] = np.sin(ang)
    right = np.zeros((128, 256))
    right[:64, :128] = lanes
    right[64:, 128:] = lanes
    right_hi, right_lo = np_split(right)
    rows = np.zeros((ROWS, BOX))
    rows[:33] = np.cos(ang).T / BOX
    rows[HALF : HALF + 33] = np.sin(ang).T / BOX
    left_hi, left_lo = np_split(rows)
    left = np.concatenate([left_hi, left_hi, left_lo], 1)
    phi = np.where(freq % 32 == 0, 0.5, 1.0)
    both = -4.0 / (NT * NP) * phi[:, None] * phi[None, :]
    plus, minus = both.copy(), both.copy()
    plus[31, 31] *= 2.0
    minus[31, 31] = 0.0
    aux = np.zeros((3, HALF, 128), np.float32)
    for base in (0, 64):
        aux[0, :33, base : base + 33] = freq[:, None] ** 2 + freq[None, :] ** 2
        aux[1, :33, base : base + 33] = plus
        aux[2, :33, base : base + 33] = minus
    joiner = np.zeros((256, 2 * ROWS), jnp.bfloat16)
    chooser = np.zeros((ROWS, 128), jnp.bfloat16)
    for i in range(HALF):
        for part in (0, 1):
            joiner[128 * part + i, ROWS * part + i] = 1
            joiner[128 * part + 64 + i, ROWS * part + HALF + i] = 1
        chooser[i, i] = 1
        chooser[HALF + i, 64 + i] = 1
    return right_hi, right_lo, left, joiner, chooser, aux


def cut_kernel(anchor, angle, focus, warp, image, out, held, sem, strip):
    bands = [pl.ds(i * (IMG // 8), IMG // 8) for i in range(8)]
    copies = [
        pltpu.make_async_copy(image.at[0, 0, band], held.at[band], sem.at[i])
        for i, band in enumerate(bands)
    ]
    for copy in copies:
        copy.start()
    lane = lax.broadcasted_iota(jnp.int32, (8, 128), 1)
    sub = lax.broadcasted_iota(jnp.int32, (8, 128), 0)
    values = [angle[0, 0], focus[0, 0]] + [warp[0, 0, i] for i in range(6)]
    row = jnp.zeros((8, 128), F32)
    for i, v in enumerate(values):
        row = jnp.where(lane == i, v, row)
    hi = row.astype(BF16).astype(F32)
    mid = (row - hi).astype(BF16).astype(F32)
    low = row - hi - mid
    parts = jnp.where(sub == 0, hi, jnp.where(sub == 1, mid, jnp.where(sub == 2, low, 0.0)))
    left_half = lax.broadcasted_iota(jnp.int32, (32, 128), 1) < BOX

    for copy in copies:
        copy.wait()

    def one(p, carry):
        r, c = anchor[0, 0, 0, p], anchor[0, 0, 1, p]
        r0 = pl.multiple_of(jnp.minimum((r // 16) * 16, IMG - 80), 16)
        c0 = pl.multiple_of(jnp.minimum((c // 128) * 128, IMG - 256), 128)
        window = held[pl.ds(r0, 80), pl.ds(c0, 256)].astype(F32)
        turned = pltpu.roll(window, 256 - (c - c0), 1)[:, :128]
        strip[p % 8] = turned
        upper = strip[p % 8, pl.ds(r - r0, 32), :]
        lower = strip[p % 8, pl.ds(r - r0 + 32, 32), :]
        packed = jnp.where(left_half, upper, pltpu.roll(lower, 64, 1))
        out[p] = jnp.concatenate([packed, parts], 0).astype(BF16)
        return carry

    lax.fori_loop(0, NP, one, 0, unroll=8)


def cut(images, anchors, angle, focus, warp):
    smem = pl.BlockSpec(memory_space=pltpu.SMEM)
    return pl.pallas_call(
        cut_kernel,
        out_shape=jax.ShapeDtypeStruct((NP, 40, 128), BF16),
        in_specs=[smem, smem, smem, smem, pl.BlockSpec(memory_space=pl.ANY)],
        out_specs=pl.BlockSpec(memory_space=pltpu.VMEM),
        scratch_shapes=[
            pltpu.VMEM((IMG, IMG), BF16),
            pltpu.SemaphoreType.DMA((8,)),
            pltpu.VMEM((8, 80, 128), F32),
        ],
        compiler_params=pltpu.CompilerParams(vmem_limit_bytes=55 << 20),
    )(jnp.transpose(anchors, (0, 1, 3, 2)), angle, focus, warp, images)


def work_kernel(
    slot,
    euler,
    incoming,
    centers,
    amplitudes,
    widths,
    right_hi,
    right_lo,
    left,
    joiner,
    chooser,
    aux,
    out,
    xs,
    base,
    step,
    zero,
    env,
    acc,
    model,
    spectra,
    mats,
    focus,
    cols,
    received,
    raw,
    sem,
):
    copy = pltpu.make_async_copy(incoming, received, sem)
    copy.start()
    copy.wait()
    raw[...] = received[:, 32:40, :].astype(F32).reshape(NT * 8, 128)
    prm = raw[pl.ds(0, NT, stride=8), :] + raw[pl.ds(1, NT, stride=8), :]
    prm = prm + raw[pl.ds(2, NT, stride=8), :]
    focus[...] = jnp.broadcast_to(prm[:, 1:2], (NT, 128))
    ct, st = cos_sin_turns(prm * (0.5 / math.pi))
    firsts = (ct[:, 0:1], st[:, 0:1])
    rest = (1.0 + prm[:, 2:3], prm[:, 3:4], prm[:, 4:5], 1.0 + prm[:, 5:6])
    shifts = (20.0 * prm[:, 6:7], 20.0 * prm[:, 7:8])
    for i, column in enumerate(firsts + rest + shifts):
        cols[i] = jnp.broadcast_to(column, (NT, 128))
    mine = slot[0]
    turn = []
    for i in range(3):
        angle = jnp.full((8, 128), euler[i, 0, mine], F32)
        c, s = cos_sin_turns(angle * (0.5 / math.pi))
        turn.append((c[0:1, 0:1], s[0:1, 0:1]))
    (ca, sa), (cb, sb), (cc, sc) = turn

    def rotated(sl):
        x, y, z = centers[0:1, sl], centers[1:2, sl], centers[2:3, sl]
        x, y = cc * x - sc * y, sc * x + cc * y
        x, z = cb * x + sb * z, cb * z - sb * x
        x, y = ca * x - sa * y, sa * x + ca * y
        return x, y, z

    blur = 2.0 * math.pi**2 / BOX**2
    freq8 = lax.broadcasted_iota(jnp.int32, (8, CH), 0).astype(F32) + 1.0
    freq32 = lax.broadcasted_iota(jnp.int32, (32, CH), 0).astype(F32) + 1.0
    first = lax.broadcasted_iota(jnp.int32, (8, CH), 0) == 0

    lane = lax.broadcasted_iota(jnp.int32, (HALF, 128), 1)
    sign = jnp.where(lane < 64, 1.0, -1.0)

    def swap(x):
        return pltpu.roll(x, 64, 1)

    def spectrum(c, sums):
        rows = received[pl.ds(c * 4, 4), 0:32, :].reshape(128, 128)
        halves = jnp.dot(rows, right_hi[...], preferred_element_type=F32)
        halves = halves + jnp.dot(rows, right_lo[...], preferred_element_type=F32)
        for i in range(4):
            z = halves[32 * i : 32 * i + 32]
            z = jnp.concatenate([z[:, :128], z[:, 128:]], 0)
            z_hi, z_lo = split(z)
            p = jnp.dot(
                left[...], jnp.concatenate([z_hi, z_lo, z_hi], 0), preferred_element_type=F32
            )
            pc, ps = p[:HALF], swap(p[HALF:])
            spectra[c * 4 + i, :HALF] = pc
            spectra[c * 4 + i, HALF:] = ps
            plus, minus = sign * pc - ps, pc + sign * ps
            sums = sums[0] + plus * plus, sums[1] + minus * minus
        return sums

    def prepare(c, sums):
        sl = pl.ds(pl.multiple_of(c * CH, CH), CH)
        r0, r1, r2 = rotated(sl)
        ct, st, a00, a01, a10, a11, sh_x, sh_y = (
            jnp.concatenate([cols[i]] * (CH // 128), 1) for i in range(8)
        )
        px = ct * r0 + st * r2
        ux = (a00 * px + a01 * r1 + sh_x) * (1.0 / BOX) + 0.5
        uy = (a10 * px + a11 * r1 + sh_y) * (1.0 / BOX) + 0.5
        wide = -blur * widths[0:1, sl] * widths[0:1, sl]
        damp = jnp.exp(wide * (freq32 * freq32))
        env[0, :, sl] = damp
        env[1, :, sl] = amplitudes[0:1, sl] * damp
        zero[0, :, sl] = jnp.where(first, 1.0, 0.0)
        zero[1, :, sl] = jnp.where(first, amplitudes[0:1, sl], 0.0)
        for axis, u in ((0, ux), (1, uy)):
            u = u - jnp.round(u)
            c1, s1 = cos_sin_turns(u)
            def twice(p):
                return 1.0 - 2.0 * (p[1] * p[1]), 2.0 * (p[0] * p[1])

            def times(p, q):
                return p[0] * q[0] - p[1] * q[1], p[0] * q[1] + p[1] * q[0]

            e1 = (c1, s1)
            e2 = twice(e1)
            e3 = times(e2, e1)
            e4 = twice(e2)
            e5 = times(e4, e1)
            e6 = twice(e3)
            e7 = times(e4, e3)
            c8, s8 = e8 = twice(e4)
            step[2 * axis, :, sl] = c8
            step[2 * axis + 1, :, sl] = s8
            for j, e in enumerate((e1, e2, e3, e4, e5, e6, e7, e8)):
                for i in range(CH // 128):
                    tile = c * (CH // 128) + i
                    lanes = slice(i * 128, i * 128 + 128)
                    base[2 * axis, tile, pl.ds(j, NT, stride=8), :] = e[0][:, lanes]
                    base[2 * axis + 1, tile, pl.ds(j, NT, stride=8), :] = e[1][:, lanes]
        return spectrum(c, sums)

    nought = jnp.zeros((HALF, 128), F32)
    plus, minus = lax.fori_loop(0, NCH, prepare, (nought, nought), unroll=2)
    f_plus = aux[1] / (0.25 + (plus + swap(plus)) * (1.0 / NT))
    f_minus = aux[2] / (0.25 + (minus + swap(minus)) * (1.0 / NT))
    radius = aux[0]

    blank = jnp.zeros((24, CH), F32)

    def factors(k, axis, c):
        sl = slice(c * CH, (c + 1) * CH)
        k8 = pl.multiple_of(k * 8, 8)
        tiles = range(c * (CH // 128), (c + 1) * (CH // 128))
        gc = jnp.concatenate([base[2 * axis, t, pl.ds(k8, 8), :] for t in tiles], 1)
        gs = jnp.concatenate([base[2 * axis + 1, t, pl.ds(k8, 8), :] for t in tiles], 1)
        rc = step[2 * axis, pl.ds(k, 1), sl]
        rs = step[2 * axis + 1, pl.ds(k, 1), sl]
        cs, ss = [], []
        for m in range(4):
            damp = env[axis, 8 * m : 8 * m + 8, sl]
            cm, sm = damp * gc, damp * gs
            xs[k, axis * 64 + 8 * m : axis * 64 + 8 * m + 8, sl] = cm
            xs[k, axis * 64 + 32 + 8 * m : axis * 64 + 40 + 8 * m, sl] = sm
            cs.append(cm)
            ss.append(sm)
            if m < 3:
                gc, gs = gc * rc - gs * rs, gc * rs + gs * rc
        return cs, ss

    def forward(b):
        total = jnp.zeros((144, 256), F32)
        for c in range(NCH):
            sl = slice(c * CH, (c + 1) * CH)
            left_rows, right_rows = [], []
            for k in (2 * b, 2 * b + 1):
                cs, ss = factors(k, 0, c)
                left_rows += cs + ss
                cs, ss = factors(k, 1, c)
                right_rows += cs + [zero[1, :, sl], blank] + ss + [blank, blank[:8]]
            left_rows += [zero[0, :, sl], blank[:8]]
            total = total + lax.dot_general(
                jnp.concatenate(left_rows, 0).astype(BF16),
                jnp.concatenate(right_rows, 0).astype(BF16),
                (((1,), (1,)), ((), ())),
                preferred_element_type=F32,
            )
        for i in range(2):
            lanes = slice(128 * i, 128 * i + 128)
            model[2 * b + i, :32] = total[64 * i : 64 * i + 32, lanes]
            model[2 * b + i, 32:HALF] = total[128:136, lanes]
            model[2 * b + i, HALF : HALF + 32] = total[64 * i + 32 : 64 * i + 64, lanes]
            model[2 * b + i, HALF + 32 :] = jnp.zeros((8, 128), F32)

    def residual(k):
        x = focus[pl.ds(k, 1), :] * radius * (1.0 / BOX) + 0.1
        n = jnp.round(x * (0.5 / math.pi))
        r = (x - n * 6.28125) - n * (2.0 * math.pi - 6.28125)
        ctf = -cos_sin_turns(r * (0.5 / math.pi))[1]
        dc = spectra[k, :HALF] - ctf * model[k, :HALF]
        ds = spectra[k, HALF:] - ctf * swap(model[k, HALF:])
        hp = (f_plus * ctf) * (sign * dc - ds)
        hm = (f_minus * ctf) * (dc + sign * ds)
        m1 = jnp.concatenate([hm, swap(sign * hm)], 0).astype(BF16)
        m2 = jnp.concatenate([sign * hp, -swap(hp)], 0).astype(BF16)
        back_x = jnp.dot(jnp.concatenate([m1, m2], 1), joiner[...], preferred_element_type=F32)
        back_y = lax.dot_general(
            chooser[...],
            jnp.concatenate([m1, m2], 0),
            (((1,), (1,)), ((), ())),
            preferred_element_type=F32,
        )
        for axis, back in enumerate((back_x, back_y)):
            rows = [back[:32], back[HALF : HALF + 32], back[32:HALF], back[HALF + 32 :]]
            mats[k, axis] = jnp.concatenate(rows, 0).astype(BF16)

    def pair(b, carry):
        forward(b + 1)
        residual(2 * b)
        residual(2 * b + 1)
        return carry

    forward(0)
    lax.fori_loop(0, NT // 2 - 1, pair, 0, unroll=UF)
    residual(NT - 2)
    residual(NT - 1)

    acc[...] = jnp.zeros_like(acc)
    w1 = [freq8 + float(8 * m) for m in range(4)]
    w2 = [w * w for w in w1]

    def backward(k, carry):
        k8 = pl.multiple_of(k * 8, 8)
        for c in range(NCH):
            sl = slice(c * CH, (c + 1) * CH)
            sides, parts = [], []
            for axis in (0, 1):
                cs = [xs[k, axis * 64 + 8 * m : axis * 64 + 8 * m + 8, sl] for m in range(4)]
                ss = [xs[k, axis * 64 + 32 + 8 * m : axis * 64 + 40 + 8 * m, sl] for m in range(4)]
                parts.append((cs, ss))
                rows = cs + [zero[axis, :, sl]] + ss + [blank[:8]]
                sides.append(jnp.concatenate(rows, 0).astype(BF16))
            width_sum = acc[0, :, sl]
            for axis in (0, 1):
                back = jnp.dot(
                    mats[k, axis, : 64 + 16 * axis],
                    jnp.concatenate([sides[1 - axis]] * 2, 0),
                    preferred_element_type=F32,
                )
                cs, ss = parts[axis]
                move = None
                value_sum = acc[1, :, sl] if axis == 1 else None
                for m in range(4):
                    kc = back[8 * m : 8 * m + 8]
                    ks = back[32 + 8 * m : 40 + 8 * m]
                    re = cs[m] * kc + ss[m] * ks
                    im = w1[m] * (cs[m] * ks - ss[m] * kc)
                    width_sum = width_sum + w2[m] * re
                    move = im if m == 0 else move + im
                    if axis == 1:
                        value_sum = value_sum + re
                if axis == 1:
                    acc[1, :, sl] = value_sum + zero[1, :, sl] * back[64:72]
                for t in range(CH // 128):
                    lanes = slice(t * 128, t * 128 + 128)
                    base[axis, c * (CH // 128) + t, pl.ds(k8, 8), :] = move[:, lanes]
            acc[0, :, sl] = width_sum
        return carry

    lax.fori_loop(0, NT, backward, 0, unroll=UB)

    terms = [jnp.zeros((NT, 128), F32) for _ in range(6)]
    unit = 2.0 * math.pi / BOX
    ct, st, a00, a01, a10, a11 = (cols[i] for i in range(6))
    for c in range(G // 128):
        sl = slice(c * 128, (c + 1) * 128)
        moves = []
        for axis in (0, 1):
            move = base[axis, c, pl.ds(0, NT, stride=8), :]
            for j in range(1, 8):
                move = move + base[axis, c, pl.ds(j, NT, stride=8), :]
            moves.append(unit * move)
        mx, my = moves
        r0, r1, r2 = rotated(sl)
        px = ct * r0 + st * r2
        for i, t in enumerate((mx * px, mx * r1, my * px, my * r1, mx, my)):
            terms[i] = terms[i] + t
        vx = a00 * mx + a10 * my
        vy = a01 * mx + a11 * my
        x = jnp.sum(ct * vx, axis=0, keepdims=True)
        z = jnp.sum(st * vx, axis=0, keepdims=True)
        y = jnp.sum(vy, axis=0, keepdims=True)
        x, y = ca * x + sa * y, ca * y - sa * x
        x, z = cb * x - sb * z, sb * x + cb * z
        x, y = cc * x + sc * y, cc * y - sc * x
        curve = jnp.sum(acc[0, :, sl], axis=0, keepdims=True)
        value = jnp.sum(acc[1, :, sl], axis=0, keepdims=True)
        rows = (x, y, z, value / amplitudes[0:1, sl], (-2.0 * blur) * widths[0:1, sl] * curve)
        for i, row in enumerate(rows):
            out[c, 0:1, i * CHUNK : (i + 1) * CHUNK] = row
    lane_w = lax.broadcasted_iota(jnp.int32, (NT, 128), 1)
    warp_rows = jnp.zeros((NT, 128), F32)
    for i in range(6):
        total = jnp.sum(terms[i], axis=1, keepdims=True) * (20.0 if i > 3 else 1.0)
        warp_rows = jnp.where(lane_w == i, total, warp_rows)
    moved_rows = pltpu.roll(warp_rows, 64, 1)
    for d in range(SHARES):
        k = 2 * d
        out[d, 0:1, 5 * CHUNK : 6 * CHUNK] = warp_rows[k : k + 1] + moved_rows[k + 1 : k + 2]


def work(slot, euler, received, centers, amplitudes, widths):
    smem = pl.BlockSpec(memory_space=pltpu.SMEM)
    vmem = pl.BlockSpec(memory_space=pltpu.VMEM)
    right_hi, right_lo, left, joiner, chooser, aux = tables()
    return pl.pallas_call(
        work_kernel,
        out_shape=jax.ShapeDtypeStruct((SHARES, 1, 6 * CHUNK), F32),
        in_specs=[smem, smem, pl.BlockSpec(memory_space=pl.ANY)] + [vmem] * 9,
        out_specs=vmem,
        scratch_shapes=[
            pltpu.VMEM((NT, 128, G), F32),
            pltpu.VMEM((4, G // 128, NT * 8, 128), F32),
            pltpu.VMEM((4, NT, G), F32),
            pltpu.VMEM((2, 8, G), F32),
            pltpu.VMEM((2, 32, G), F32),
            pltpu.VMEM((2, 8, G), F32),
            pltpu.VMEM((NT, ROWS, 128), F32),
            pltpu.VMEM((NT, ROWS, 128), F32),
            pltpu.VMEM((NT, 2, ROWS, 2 * ROWS), BF16),
            pltpu.VMEM((NT, 128), F32),
            pltpu.VMEM((8, NT, 128), F32),
            pltpu.VMEM((NT, 40, 128), BF16),
            pltpu.VMEM((NT * 8, 128), F32),
            pltpu.SemaphoreType.DMA,
        ],
        compiler_params=pltpu.CompilerParams(vmem_limit_bytes=55 << 20),
    )(
        slot,
        jnp.transpose(euler, (1, 0, 2)),
        received,
        centers,
        amplitudes.reshape(1, G),
        widths.reshape(1, G),
        jnp.asarray(right_hi),
        jnp.asarray(right_lo),
        jnp.asarray(left),
        jnp.asarray(joiner),
        jnp.asarray(chooser),
        jnp.asarray(aux),
    )


def on_device(tilt_images, anchors, euler, tilt_angle, defocus, warp, centers, amplitudes, widths):
    tomos, cores = lax.axis_size("tomo"), lax.axis_size("tilt") // SHARES
    row = [[(t * SHARES + i) * cores + c for i in range(SHARES)] for t in range(tomos) for c in range(cores)]
    column = [[group[i] for group in row] for i in range(SHARES)]

    def swapped(value, groups):
        return lax.all_to_all(
            value, ("tomo", "tilt"), split_axis=0, concat_axis=0, tiled=True, axis_index_groups=groups
        )

    index = lax.axis_index("tilt").astype(jnp.int32)
    first = lax.axis_index("tomo").astype(jnp.int32) * cores
    at = 5 * CHUNK + (index & 1) * 64
    payload = cut(tilt_images, anchors, tilt_angle, defocus, warp)
    rest = (index, first, at, euler, centers, amplitudes, widths)
    payload, rest = lax.optimization_barrier((payload, rest))
    received = lax.all_to_all(payload, "tilt", split_axis=0, concat_axis=0, tiled=True)
    received, rest = lax.optimization_barrier((received, rest))
    index, first, at, euler, centers, amplitudes, widths = rest
    partial = work(index.reshape(1), euler, received, centers, amplitudes, widths)
    partial, first, at = lax.optimization_barrier((partial, first, at))
    share = jnp.sum(swapped(partial, row), 0, keepdims=True)
    shares = swapped(jnp.broadcast_to(share, (tomos * cores, 1, 6 * CHUNK)), column)
    total = jnp.sum(shares, 0, keepdims=True)
    chunks = swapped(jnp.broadcast_to(total, (SHARES, 1, 6 * CHUNK)), row)
    chunks, shares, first, at = lax.optimization_barrier((chunks, shares, first, at))
    template = chunks[:, 0, : 5 * CHUNK].reshape(SHARES, 5, CHUNK)
    template = jnp.transpose(template, (1, 0, 2)).reshape(5, G)
    warp_local = jnp.sum(lax.dynamic_slice(shares, (first, 0, at), (cores, 1, 6)), 0)
    return (template, warp_local.reshape(1, 1, 6))


def solution(mesh):
    placed = (
        P("tomo", "tilt", None, None),
        P("tomo", "tilt", None, None),
        P("tomo", None, None),
        P("tomo", "tilt"),
        P("tomo", "tilt"),
        P("tomo", "tilt", None),
        P(),
        P(),
        P(),
    )
    return jax.shard_map(
        on_device,
        mesh=mesh,
        in_specs=placed,
        out_specs=(P(), P("tomo", "tilt", None)),
        check_vma=False,
    )
```

```python
import math

import jax
import jax.numpy as jnp
import numpy as np
from jax import lax
from jax.experimental import pallas as pl
from jax.experimental.pallas import tpu as pltpu
from jax.sharding import PartitionSpec as P

G = 2048
BOX = 64
IMG = 1024
NT = 32
NP = 32
SHARES = 16
CHUNK = G // SHARES
CH = 256
NCH = G // CH
HALF = 40
ROWS = 2 * HALF
UF, UB = 3, 8
F32 = jnp.float32
BF16 = jnp.bfloat16


def _fit(fn, degree):
    n = 64
    nodes = 0.125 * (1 + np.cos(np.pi * (np.arange(n) + 0.5) / n))
    return [float(c) for c in np.polynomial.polynomial.polyfit(nodes, fn(np.sqrt(nodes)), degree)]


SIN_POLY = _fit(lambda u: np.sin(np.pi * u) / u, 5)
COS_POLY = _fit(lambda u: np.cos(np.pi * u), 5)


def _horner(w, coefs):
    acc = jnp.full_like(w, coefs[-1])
    for c in coefs[-2::-1]:
        acc = acc * w + c
    return acc


def cos_sin_turns(turns):
    u = turns - jnp.round(turns)
    w = u * u
    s = u * _horner(w, SIN_POLY)
    c = _horner(w, COS_POLY)
    return 1.0 - 2.0 * (s * s), 2.0 * (s * c)


def split(x):
    hi = x.astype(BF16)
    return hi, (x - hi.astype(F32)).astype(BF16)


def np_split(x):
    hi = x.astype(jnp.bfloat16)
    lo = (x - hi.astype(np.float64)).astype(jnp.bfloat16)
    return hi, lo


def tables():
    pos = np.arange(BOX)
    freq = np.append(np.arange(1, 33), 0)
    ang = 2 * np.pi * ((pos[:, None] * freq[None, :]) % BOX) / BOX
    lanes = np.zeros((BOX, 128))
    lanes[:, :33] = np.cos(ang)
    lanes[:, 64:97] = np.sin(ang)
    right = np.zeros((128, 256))
    right[:64, :128] = lanes
    right[64:, 128:] = lanes
    right_hi, right_lo = np_split(right)
    rows = np.zeros((ROWS, BOX))
    rows[:33] = np.cos(ang).T / BOX
    rows[HALF : HALF + 33] = np.sin(ang).T / BOX
    left_hi, left_lo = np_split(rows)
    left = np.concatenate([left_hi, left_hi, left_lo], 1)
    phi = np.where(freq % 32 == 0, 0.5, 1.0)
    both = -4.0 / (NT * NP) * phi[:, None] * phi[None, :]
    plus, minus = both.copy(), both.copy()
    plus[31, 31] *= 2.0
    minus[31, 31] = 0.0
    aux = np.zeros((3, HALF, 128), np.float32)
    for base in (0, 64):
        aux[0, :33, base : base + 33] = freq[:, None] ** 2 + freq[None, :] ** 2
        aux[1, :33, base : base + 33] = plus
        aux[2, :33, base : base + 33] = minus
    joiner = np.zeros((256, 2 * ROWS), jnp.bfloat16)
    chooser = np.zeros((ROWS, 128), jnp.bfloat16)
    for i in range(HALF):
        for part in (0, 1):
            joiner[128 * part + i, ROWS * part + i] = 1
            joiner[128 * part + 64 + i, ROWS * part + HALF + i] = 1
        chooser[i, i] = 1
        chooser[HALF + i, 64 + i] = 1
    return right_hi, right_lo, left, joiner, chooser, aux


def cut_kernel(anchor, angle, focus, warp, image, out, held, sem, strip):
    bands = [pl.ds(i * (IMG // 8), IMG // 8) for i in range(8)]
    copies = [
        pltpu.make_async_copy(image.at[0, 0, band], held.at[band], sem.at[i])
        for i, band in enumerate(bands)
    ]
    for copy in copies:
        copy.start()
    lane = lax.broadcasted_iota(jnp.int32, (8, 128), 1)
    sub = lax.broadcasted_iota(jnp.int32, (8, 128), 0)
    values = [angle[0, 0], focus[0, 0]] + [warp[0, 0, i] for i in range(6)]
    row = jnp.zeros((8, 128), F32)
    for i, v in enumerate(values):
        row = jnp.where(lane == i, v, row)
    hi = row.astype(BF16).astype(F32)
    mid = (row - hi).astype(BF16).astype(F32)
    low = row - hi - mid
    parts = jnp.where(sub == 0, hi, jnp.where(sub == 1, mid, jnp.where(sub == 2, low, 0.0)))
    left_half = lax.broadcasted_iota(jnp.int32, (32, 128), 1) < BOX

    for copy in copies:
        copy.wait()

    def one(p, carry):
        r, c = anchor[0, 0, 0, p], anchor[0, 0, 1, p]
        r0 = pl.multiple_of(jnp.minimum((r // 16) * 16, IMG - 80), 16)
        c0 = pl.multiple_of(jnp.minimum((c // 128) * 128, IMG - 256), 128)
        window = held[pl.ds(r0, 80), pl.ds(c0, 256)].astype(F32)
        turned = pltpu.roll(window, 256 - (c - c0), 1)[:, :128]
        strip[p % 8] = turned
        upper = strip[p % 8, pl.ds(r - r0, 32), :]
        lower = strip[p % 8, pl.ds(r - r0 + 32, 32), :]
        packed = jnp.where(left_half, upper, pltpu.roll(lower, 64, 1))
        out[p] = jnp.concatenate([packed, parts], 0).astype(BF16)
        return carry

    lax.fori_loop(0, NP, one, 0, unroll=8)


def cut(images, anchors, angle, focus, warp):
    smem = pl.BlockSpec(memory_space=pltpu.SMEM)
    return pl.pallas_call(
        cut_kernel,
        out_shape=jax.ShapeDtypeStruct((NP, 40, 128), BF16),
        in_specs=[smem, smem, smem, smem, pl.BlockSpec(memory_space=pl.ANY)],
        out_specs=pl.BlockSpec(memory_space=pltpu.VMEM),
        scratch_shapes=[
            pltpu.VMEM((IMG, IMG), BF16),
            pltpu.SemaphoreType.DMA((8,)),
            pltpu.VMEM((8, 80, 128), F32),
        ],
        compiler_params=pltpu.CompilerParams(vmem_limit_bytes=55 << 20),
    )(jnp.transpose(anchors, (0, 1, 3, 2)), angle, focus, warp, images)


def work_kernel(
    slot,
    euler,
    incoming,
    centers,
    amplitudes,
    widths,
    right_hi,
    right_lo,
    left,
    joiner,
    chooser,
    aux,
    out,
    xs,
    base,
    step,
    zero,
    env,
    acc,
    model,
    spectra,
    mats,
    focus,
    cols,
    received,
    raw,
    sem,
):
    copy = pltpu.make_async_copy(incoming, received, sem)
    copy.start()
    copy.wait()
    raw[...] = received[:, 32:40, :].astype(F32).reshape(NT * 8, 128)
    prm = raw[pl.ds(0, NT, stride=8), :] + raw[pl.ds(1, NT, stride=8), :]
    prm = prm + raw[pl.ds(2, NT, stride=8), :]
    focus[...] = jnp.broadcast_to(prm[:, 1:2], (NT, 128))
    ct, st = cos_sin_turns(prm * (0.5 / math.pi))
    firsts = (ct[:, 0:1], st[:, 0:1])
    rest = (1.0 + prm[:, 2:3], prm[:, 3:4], prm[:, 4:5], 1.0 + prm[:, 5:6])
    shifts = (20.0 * prm[:, 6:7], 20.0 * prm[:, 7:8])
    for i, column in enumerate(firsts + rest + shifts):
        cols[i] = jnp.broadcast_to(column, (NT, 128))
    mine = slot[0]
    turn = []
    for i in range(3):
        angle = jnp.full((8, 128), euler[i, 0, mine], F32)
        c, s = cos_sin_turns(angle * (0.5 / math.pi))
        turn.append((c[0:1, 0:1], s[0:1, 0:1]))
    (ca, sa), (cb, sb), (cc, sc) = turn

    def rotated(sl):
        x, y, z = centers[0:1, sl], centers[1:2, sl], centers[2:3, sl]
        x, y = cc * x - sc * y, sc * x + cc * y
        x, z = cb * x + sb * z, cb * z - sb * x
        x, y = ca * x - sa * y, sa * x + ca * y
        return x, y, z

    blur = 2.0 * math.pi**2 / BOX**2
    freq8 = lax.broadcasted_iota(jnp.int32, (8, CH), 0).astype(F32) + 1.0
    freq32 = lax.broadcasted_iota(jnp.int32, (32, CH), 0).astype(F32) + 1.0
    first = lax.broadcasted_iota(jnp.int32, (8, CH), 0) == 0

    lane = lax.broadcasted_iota(jnp.int32, (HALF, 128), 1)
    sign = jnp.where(lane < 64, 1.0, -1.0)

    def swap(x):
        return pltpu.roll(x, 64, 1)

    def spectrum(c, sums):
        rows = received[pl.ds(c * 4, 4), 0:32, :].reshape(128, 128)
        halves = jnp.dot(rows, right_hi[...], preferred_element_type=F32)
        halves = halves + jnp.dot(rows, right_lo[...], preferred_element_type=F32)
        for i in range(4):
            z = halves[32 * i : 32 * i + 32]
            z = jnp.concatenate([z[:, :128], z[:, 128:]], 0)
            z_hi, z_lo = split(z)
            p = jnp.dot(
                left[...], jnp.concatenate([z_hi, z_lo, z_hi], 0), preferred_element_type=F32
            )
            pc, ps = p[:HALF], swap(p[HALF:])
            spectra[c * 4 + i, :HALF] = pc
            spectra[c * 4 + i, HALF:] = ps
            plus, minus = sign * pc - ps, pc + sign * ps
            sums = sums[0] + plus * plus, sums[1] + minus * minus
        return sums

    def prepare(c, sums):
        sl = pl.ds(pl.multiple_of(c * CH, CH), CH)
        r0, r1, r2 = rotated(sl)
        ct, st, a00, a01, a10, a11, sh_x, sh_y = (
            jnp.concatenate([cols[i]] * (CH // 128), 1) for i in range(8)
        )
        px = ct * r0 + st * r2
        ux = (a00 * px + a01 * r1 + sh_x) * (1.0 / BOX) + 0.5
        uy = (a10 * px + a11 * r1 + sh_y) * (1.0 / BOX) + 0.5
        wide = -blur * widths[0:1, sl] * widths[0:1, sl]
        damp = jnp.exp(wide * (freq32 * freq32))
        env[0, :, sl] = damp
        env[1, :, sl] = amplitudes[0:1, sl] * damp
        zero[0, :, sl] = jnp.where(first, 1.0, 0.0)
        zero[1, :, sl] = jnp.where(first, amplitudes[0:1, sl], 0.0)
        for axis, u in ((0, ux), (1, uy)):
            u = u - jnp.round(u)
            c1, s1 = cos_sin_turns(u)
            def twice(p):
                return 1.0 - 2.0 * (p[1] * p[1]), 2.0 * (p[0] * p[1])

            def times(p, q):
                return p[0] * q[0] - p[1] * q[1], p[0] * q[1] + p[1] * q[0]

            e1 = (c1, s1)
            e2 = twice(e1)
            e3 = times(e2, e1)
            e4 = twice(e2)
            e5 = times(e4, e1)
            e6 = twice(e3)
            e7 = times(e4, e3)
            c8, s8 = e8 = twice(e4)
            step[2 * axis, :, sl] = c8
            step[2 * axis + 1, :, sl] = s8
            for j, e in enumerate((e1, e2, e3, e4, e5, e6, e7, e8)):
                for i in range(CH // 128):
                    tile = c * (CH // 128) + i
                    lanes = slice(i * 128, i * 128 + 128)
                    base[2 * axis, tile, pl.ds(j, NT, stride=8), :] = e[0][:, lanes]
                    base[2 * axis + 1, tile, pl.ds(j, NT, stride=8), :] = e[1][:, lanes]
        return spectrum(c, sums)

    nought = jnp.zeros((HALF, 128), F32)
    plus, minus = lax.fori_loop(0, NCH, prepare, (nought, nought), unroll=NCH)
    f_plus = aux[1] / (0.25 + (plus + swap(plus)) * (1.0 / NT))
    f_minus = aux[2] / (0.25 + (minus + swap(minus)) * (1.0 / NT))
    radius = aux[0]

    blank = jnp.zeros((24, CH), F32)

    def factors(k, axis, c):
        sl = slice(c * CH, (c + 1) * CH)
        k8 = pl.multiple_of(k * 8, 8)
        tiles = range(c * (CH // 128), (c + 1) * (CH // 128))
        gc = jnp.concatenate([base[2 * axis, t, pl.ds(k8, 8), :] for t in tiles], 1)
        gs = jnp.concatenate([base[2 * axis + 1, t, pl.ds(k8, 8), :] for t in tiles], 1)
        rc = step[2 * axis, pl.ds(k, 1), sl]
        rs = step[2 * axis + 1, pl.ds(k, 1), sl]
        cs, ss = [], []
        for m in range(4):
            damp = env[axis, 8 * m : 8 * m + 8, sl]
            cm, sm = damp * gc, damp * gs
            xs[k, axis * 64 + 8 * m : axis * 64 + 8 * m + 8, sl] = cm
            xs[k, axis * 64 + 32 + 8 * m : axis * 64 + 40 + 8 * m, sl] = sm
            cs.append(cm)
            ss.append(sm)
            if m < 3:
                gc, gs = gc * rc - gs * rs, gc * rs + gs * rc
        return cs, ss

    def forward(b):
        total = jnp.zeros((144, 256), F32)
        for c in range(NCH):
            sl = slice(c * CH, (c + 1) * CH)
            left_rows, right_rows = [], []
            for k in (2 * b, 2 * b + 1):
                cs, ss = factors(k, 0, c)
                left_rows += cs + ss
                cs, ss = factors(k, 1, c)
                right_rows += cs + [zero[1, :, sl], blank] + ss + [blank, blank[:8]]
            left_rows += [zero[0, :, sl], blank[:8]]
            total = total + lax.dot_general(
                jnp.concatenate(left_rows, 0).astype(BF16),
                jnp.concatenate(right_rows, 0).astype(BF16),
                (((1,), (1,)), ((), ())),
                preferred_element_type=F32,
            )
        for i in range(2):
            lanes = slice(128 * i, 128 * i + 128)
            model[2 * b + i, :32] = total[64 * i : 64 * i + 32, lanes]
            model[2 * b + i, 32:HALF] = total[128:136, lanes]
            model[2 * b + i, HALF : HALF + 32] = total[64 * i + 32 : 64 * i + 64, lanes]
            model[2 * b + i, HALF + 32 :] = jnp.zeros((8, 128), F32)

    def residual(k):
        x = focus[pl.ds(k, 1), :] * radius * (1.0 / BOX) + 0.1
        n = jnp.round(x * (0.5 / math.pi))
        r = (x - n * 6.28125) - n * (2.0 * math.pi - 6.28125)
        ctf = -cos_sin_turns(r * (0.5 / math.pi))[1]
        dc = spectra[k, :HALF] - ctf * model[k, :HALF]
        ds = spectra[k, HALF:] - ctf * swap(model[k, HALF:])
        hp = (f_plus * ctf) * (sign * dc - ds)
        hm = (f_minus * ctf) * (dc + sign * ds)
        m1 = jnp.concatenate([hm, swap(sign * hm)], 0).astype(BF16)
        m2 = jnp.concatenate([sign * hp, -swap(hp)], 0).astype(BF16)
        back_x = jnp.dot(jnp.concatenate([m1, m2], 1), joiner[...], preferred_element_type=F32)
        back_y = lax.dot_general(
            chooser[...],
            jnp.concatenate([m1, m2], 0),
            (((1,), (1,)), ((), ())),
            preferred_element_type=F32,
        )
        for axis, back in enumerate((back_x, back_y)):
            rows = [back[:32], back[HALF : HALF + 32], back[32:HALF], back[HALF + 32 :]]
            mats[k, axis] = jnp.concatenate(rows, 0).astype(BF16)

    def pair(b, carry):
        forward(b + 1)
        residual(2 * b)
        residual(2 * b + 1)
        return carry

    forward(0)
    lax.fori_loop(0, NT // 2 - 1, pair, 0, unroll=UF)
    residual(NT - 2)
    residual(NT - 1)

    acc[...] = jnp.zeros_like(acc)
    w1 = [freq8 + float(8 * m) for m in range(4)]
    w2 = [w * w for w in w1]

    def backward(k, carry):
        k8 = pl.multiple_of(k * 8, 8)
        for c in range(NCH):
            sl = slice(c * CH, (c + 1) * CH)
            sides, parts = [], []
            for axis in (0, 1):
                cs = [xs[k, axis * 64 + 8 * m : axis * 64 + 8 * m + 8, sl] for m in range(4)]
                ss = [xs[k, axis * 64 + 32 + 8 * m : axis * 64 + 40 + 8 * m, sl] for m in range(4)]
                parts.append((cs, ss))
                rows = cs + [zero[axis, :, sl]] + ss + [blank[:8]]
                sides.append(jnp.concatenate(rows, 0).astype(BF16))
            width_sum = acc[0, :, sl]
            for axis in (0, 1):
                back = jnp.dot(
                    mats[k, axis, : 64 + 16 * axis],
                    jnp.concatenate([sides[1 - axis]] * 2, 0),
                    preferred_element_type=F32,
                )
                cs, ss = parts[axis]
                move = None
                value_sum = acc[1, :, sl] if axis == 1 else None
                for m in range(4):
                    kc = back[8 * m : 8 * m + 8]
                    ks = back[32 + 8 * m : 40 + 8 * m]
                    re = cs[m] * kc + ss[m] * ks
                    im = w1[m] * (cs[m] * ks - ss[m] * kc)
                    width_sum = width_sum + w2[m] * re
                    move = im if m == 0 else move + im
                    if axis == 1:
                        value_sum = value_sum + re
                if axis == 1:
                    acc[1, :, sl] = value_sum + zero[1, :, sl] * back[64:72]
                for t in range(CH // 128):
                    lanes = slice(t * 128, t * 128 + 128)
                    base[axis, c * (CH // 128) + t, pl.ds(k8, 8), :] = move[:, lanes]
            acc[0, :, sl] = width_sum
        return carry

    lax.fori_loop(0, NT, backward, 0, unroll=UB)

    terms = [jnp.zeros((NT, 128), F32) for _ in range(6)]
    unit = 2.0 * math.pi / BOX
    ct, st, a00, a01, a10, a11 = (cols[i] for i in range(6))
    for c in range(G // 128):
        sl = slice(c * 128, (c + 1) * 128)
        moves = []
        for axis in (0, 1):
            move = base[axis, c, pl.ds(0, NT, stride=8), :]
            for j in range(1, 8):
                move = move + base[axis, c, pl.ds(j, NT, stride=8), :]
            moves.append(unit * move)
        mx, my = moves
        r0, r1, r2 = rotated(sl)
        px = ct * r0 + st * r2
        for i, t in enumerate((mx * px, mx * r1, my * px, my * r1, mx, my)):
            terms[i] = terms[i] + t
        vx = a00 * mx + a10 * my
        vy = a01 * mx + a11 * my
        x = jnp.sum(ct * vx, axis=0, keepdims=True)
        z = jnp.sum(st * vx, axis=0, keepdims=True)
        y = jnp.sum(vy, axis=0, keepdims=True)
        x, y = ca * x + sa * y, ca * y - sa * x
        x, z = cb * x - sb * z, sb * x + cb * z
        x, y = cc * x + sc * y, cc * y - sc * x
        curve = jnp.sum(acc[0, :, sl], axis=0, keepdims=True)
        value = jnp.sum(acc[1, :, sl], axis=0, keepdims=True)
        rows = (x, y, z, value / amplitudes[0:1, sl], (-2.0 * blur) * widths[0:1, sl] * curve)
        for i, row in enumerate(rows):
            out[c, 0:1, i * CHUNK : (i + 1) * CHUNK] = row
    lane_w = lax.broadcasted_iota(jnp.int32, (NT, 128), 1)
    warp_rows = jnp.zeros((NT, 128), F32)
    for i in range(6):
        total = jnp.sum(terms[i], axis=1, keepdims=True) * (20.0 if i > 3 else 1.0)
        warp_rows = jnp.where(lane_w == i, total, warp_rows)
    moved_rows = pltpu.roll(warp_rows, 64, 1)
    for d in range(SHARES):
        k = 2 * d
        out[d, 0:1, 5 * CHUNK : 6 * CHUNK] = warp_rows[k : k + 1] + moved_rows[k + 1 : k + 2]


def work(slot, euler, received, centers, amplitudes, widths):
    smem = pl.BlockSpec(memory_space=pltpu.SMEM)
    vmem = pl.BlockSpec(memory_space=pltpu.VMEM)
    right_hi, right_lo, left, joiner, chooser, aux = tables()
    return pl.pallas_call(
        work_kernel,
        out_shape=jax.ShapeDtypeStruct((SHARES, 1, 6 * CHUNK), F32),
        in_specs=[smem, smem, pl.BlockSpec(memory_space=pl.ANY)] + [vmem] * 9,
        out_specs=vmem,
        scratch_shapes=[
            pltpu.VMEM((NT, 128, G), F32),
            pltpu.VMEM((4, G // 128, NT * 8, 128), F32),
            pltpu.VMEM((4, NT, G), F32),
            pltpu.VMEM((2, 8, G), F32),
            pltpu.VMEM((2, 32, G), F32),
            pltpu.VMEM((2, 8, G), F32),
            pltpu.VMEM((NT, ROWS, 128), F32),
            pltpu.VMEM((NT, ROWS, 128), F32),
            pltpu.VMEM((NT, 2, ROWS, 2 * ROWS), BF16),
            pltpu.VMEM((NT, 128), F32),
            pltpu.VMEM((8, NT, 128), F32),
            pltpu.VMEM((NT, 40, 128), BF16),
            pltpu.VMEM((NT * 8, 128), F32),
            pltpu.SemaphoreType.DMA,
        ],
        compiler_params=pltpu.CompilerParams(vmem_limit_bytes=55 << 20),
    )(
        slot,
        jnp.transpose(euler, (1, 0, 2)),
        received,
        centers,
        amplitudes.reshape(1, G),
        widths.reshape(1, G),
        jnp.asarray(right_hi),
        jnp.asarray(right_lo),
        jnp.asarray(left),
        jnp.asarray(joiner),
        jnp.asarray(chooser),
        jnp.asarray(aux),
    )


def on_device(tilt_images, anchors, euler, tilt_angle, defocus, warp, centers, amplitudes, widths):
    tomos, cores = lax.axis_size("tomo"), lax.axis_size("tilt") // SHARES
    row = [[(t * SHARES + i) * cores + c for i in range(SHARES)] for t in range(tomos) for c in range(cores)]
    column = [[group[i] for group in row] for i in range(SHARES)]

    def swapped(value, groups):
        return lax.all_to_all(
            value, ("tomo", "tilt"), split_axis=0, concat_axis=0, tiled=True, axis_index_groups=groups
        )

    index = lax.axis_index("tilt").astype(jnp.int32)
    first = lax.axis_index("tomo").astype(jnp.int32) * cores
    at = 5 * CHUNK + (index & 1) * 64
    payload = cut(tilt_images, anchors, tilt_angle, defocus, warp)
    rest = (index, first, at, euler, centers, amplitudes, widths)
    payload, rest = lax.optimization_barrier((payload, rest))
    received = lax.all_to_all(payload, "tilt", split_axis=0, concat_axis=0, tiled=True)
    received, rest = lax.optimization_barrier((received, rest))
    index, first, at, euler, centers, amplitudes, widths = rest
    partial = work(index.reshape(1), euler, received, centers, amplitudes, widths)
    partial, first, at = lax.optimization_barrier((partial, first, at))
    share = jnp.sum(swapped(partial, row), 0, keepdims=True)
    shares = swapped(jnp.broadcast_to(share, (tomos * cores, 1, 6 * CHUNK)), column)
    total = jnp.sum(shares, 0, keepdims=True)
    chunks = swapped(jnp.broadcast_to(total, (SHARES, 1, 6 * CHUNK)), row)
    chunks, shares, first, at = lax.optimization_barrier((chunks, shares, first, at))
    template = chunks[:, 0, : 5 * CHUNK].reshape(SHARES, 5, CHUNK)
    template = jnp.transpose(template, (1, 0, 2)).reshape(5, G)
    warp_local = jnp.sum(lax.dynamic_slice(shares, (first, 0, at), (cores, 1, 6)), 0)
    return (template, warp_local.reshape(1, 1, 6))


def solution(mesh):
    placed = (
        P("tomo", "tilt", None, None),
        P("tomo", "tilt", None, None),
        P("tomo", None, None),
        P("tomo", "tilt"),
        P("tomo", "tilt"),
        P("tomo", "tilt", None),
        P(),
        P(),
        P(),
    )
    return jax.shard_map(
        on_device,
        mesh=mesh,
        in_specs=placed,
        out_specs=(P(), P("tomo", "tilt", None)),
        check_vma=False,
    )
```
